32 devices in a mesh: rows: 8 (over z, x), cols: 4 (over y, core).
Axes of the slice: x: 2, y: 2, z: 4, core: 2. Of those that a mesh axis runs over, the one named last changes fastest.
Arguments:
- pin_feats: bfloat16 [4096, 1024], P('rows', 'cols'), may hold values from -6 to 6
- board_feats: bfloat16 [4096, 512], P('rows', 'cols'), may hold values from -6 to 6
- node_kinds: int32 [4096], P('rows'), may hold values from 0 to 1
- neighbours: int32 [4096, 50], P('rows'), may hold values from 0 to 2047
- visit_counts: int32 [4096, 50], P('rows'), may hold values from 1 to 32
- pull_rows: int32 [8, 2048], P('rows'), may hold values from 0 to 511, as said below
- proj_weight: bfloat16 [512, 1024], P(None, 'cols'), may hold values from -0.25 to 0.25
- proj_bias: float32 [1024], P('cols'), may hold values from -3 to 3
- neigh_weight: bfloat16 [2, 1024, 1024], P(None, None, 'cols'), may hold values from -0.1875 to 0.1875
- neigh_bias: float32 [2, 1024], P(None, 'cols'), may hold values from -3 to 3
- combine_weight: bfloat16 [2, 2048, 1024], P(None, None, 'cols')
- combine_bias: float32 [2, 1024], P(None, 'cols'), may hold values from -3 to 3
- head_weight: bfloat16 [1024, 1024], P(None, 'cols'), may hold values from -0.1875 to 0.1875
- head_bias: float32 [1024], P('cols'), may hold values from -3 to 3
- tail_weight: bfloat16 [1024, 1024], P(None, 'cols'), may hold values from -0.1875 to 0.1875
- tail_bias: float32 [1024], P('cols'), may hold values from -3 to 3
- cotangent: bfloat16 [4096, 1024], P('rows', 'cols'), may hold values from -6 to 6
Outputs:
- embeddings: float32 [4096, 1024], P('rows', 'cols')
- grad_pin: float32 [4096, 1024], P('rows', 'cols')
- grad_board: float32 [4096, 512], P('rows', 'cols')
- grad_proj_weight: float32 [512, 1024], P('rows', 'cols')
- grad_proj_bias: float32 [1024], P('cols')
- grad_neigh_weight: float32 [2, 1024, 1024], P(None, 'rows', 'cols')
- grad_neigh_bias: float32 [2, 1024], P(None, 'cols')
- grad_combine_weight: float32 [2, 2048, 1024], P(None, 'rows', 'cols')
- grad_combine_bias: float32 [2, 1024], P(None, 'cols')
- grad_head_weight: float32 [1024, 1024], P('rows', 'cols')
- grad_head_bias: float32 [1024], P('cols')
- grad_tail_weight: float32 [1024, 1024], P('rows', 'cols')
- grad_tail_bias: float32 [1024], P('cols')
The draws below stay inside these ranges and needn't reach their ends.
Inputs may be any that keep to these rules, and one draw needn't show every extreme that they name: `pull_rows`: row r's entries s * 256 to (s + 1) * 256 - 1 are 256 distinct local row numbers of row shard s.
All inputs are finite; a program needn't handle non-finite values.
Results may differ from the reference program's by a relative error of at most 0.029.
Values may be sent and summed in bfloat16 or wider, within the bound.
No kernel may reach another device: no remote copies, remote signals or barrier semaphores. Data moves between devices by JAX's collectives and lax.ppermute only.
A program may use at most 128 MiB of HBM per device.

```python
from functools import partial
import jax
import jax.numpy as jnp
from jax import lax

D = 1024
DB = 512
K = 50
LAYERS = 2
NODE_DEV = 512
CAP = 256
POOL = 2048
NODES = 4096
N_ROWS = 8


def draw_pull_rows(key, part):
    key = jax.random.fold_in(key, 7)
    keys = jax.random.split(key, N_ROWS * N_ROWS)

    def pick_rows(one_key):
        return jax.random.permutation(one_key, NODE_DEV)[:CAP]
    picked = jax.vmap(pick_rows)(keys)
    return picked.reshape(N_ROWS, POOL).astype(jnp.int32)


def draw_combine_weight(key, part):
    key = jax.random.fold_in(key, 11)
    column = jnp.arange(D, dtype=jnp.float32) / D
    rising = jnp.exp(jnp.log(3.0) * (column - 0.5))
    base = jax.random.normal(key, (LAYERS, 2 * D, D), jnp.float32)
    return (base * rising * (2.0 * D) ** (-0.5)).astype(jnp.bfloat16)


def touch_ends(entries, stream_key, least, top_value):
    dims = entries.shape
    spot = [jax.random.randint(jax.random.fold_in(stream_key, axis), (), 0, dims[axis]) for axis in range(len(dims))]
    entries = entries.at[tuple(spot)].set(least)
    longest = dims.index(max(dims))
    spot[longest] = (spot[longest] + 1) % dims[longest]
    return entries.at[tuple(spot)].set(top_value)


def block_levels(key, shape, cuts, least, high):
    def one(dim, parts):
        steps = jax.random.uniform(jax.random.fold_in(jax.random.fold_in(key, 6), dim), (parts,), jnp.float32, least / len(cuts), high / len(cuts))
        return jnp.repeat(jnp.exp(steps), shape[dim] // parts).reshape((-1,) + (1,) * (len(shape) - dim - 1))

    factor_of = one(*cuts[0])
    for cut in cuts[1:]:
        factor_of = factor_of * one(*cut)
    return factor_of


def gaussian(key, dims, deviation, limit, shards=(), held_as=jnp.bfloat16):
    gain = block_levels(key, dims, shards, -0.22, 0.18) if shards else 1.0
    result = jax.random.normal(key, dims, jnp.float32) * deviation * gain
    return jnp.minimum(jnp.maximum(result, -limit), limit).astype(held_as)


def setup_inputs(seed: int = 0) -> dict:
    key_of = jax.random.split(jax.random.key(seed), 18)
    pin_feats = gaussian(key_of[0], (NODES, D), 1.0, 6.0, ((0, 8), (1, 4)))
    board_feats = gaussian(key_of[1], (NODES, DB), 1.0, 6.0, ((0, 8), (1, 4)))
    node_kinds = touch_ends(jax.random.randint(key_of[2], (NODES,), 0, 2), jax.random.fold_in(key_of[2], 1), 0, 1).astype(jnp.int32)
    neighbours = touch_ends(jax.random.randint(key_of[3], (NODES, K), 0, POOL), jax.random.fold_in(key_of[3], 1), 0, POOL - 1).astype(jnp.int32)
    visit_counts = touch_ends(jax.random.randint(key_of[4], (NODES, K), 1, 33), jax.random.fold_in(key_of[4], 1), 1, 32).astype(jnp.int32)
    pull_rows = draw_pull_rows(jax.random.fold_in(key_of[17], 71), 0)
    proj_weight = gaussian(key_of[6], (DB, D), DB ** -0.5, 0.25, ((1, 4),))
    proj_bias = gaussian(key_of[7], (D,), 0.5, 3.0, ((0, 4),), jnp.float32)
    neigh_weight = gaussian(key_of[8], (LAYERS, D, D), D ** -0.5, 0.1875, ((2, 4),))
    neigh_bias = gaussian(key_of[9], (LAYERS, D), 0.5, 3.0, ((1, 4),), jnp.float32)
    combine_weight = draw_combine_weight(jax.random.fold_in(key_of[17], 71), 0)
    combine_bias = gaussian(key_of[11], (LAYERS, D), 0.5, 3.0, ((1, 4),), jnp.float32)
    head_weight = gaussian(key_of[12], (D, D), D ** -0.5, 0.1875, ((1, 4),))
    head_bias = gaussian(key_of[13], (D,), 0.5, 3.0, ((0, 4),), jnp.float32)
    tail_weight = gaussian(key_of[14], (D, D), D ** -0.5, 0.1875, ((1, 4),))
    tail_bias = gaussian(key_of[15], (D,), 0.5, 3.0, ((0, 4),), jnp.float32)
    cotangent = gaussian(key_of[16], (NODES, D), 1.0, 6.0, ((0, 8), (1, 4)))
    return dict(pin_feats=pin_feats, board_feats=board_feats, node_kinds=node_kinds, neighbours=neighbours, visit_counts=visit_counts, pull_rows=pull_rows, proj_weight=proj_weight, proj_bias=proj_bias, neigh_weight=neigh_weight, neigh_bias=neigh_bias, combine_weight=combine_weight, combine_bias=combine_bias, head_weight=head_weight, head_bias=head_bias, tail_weight=tail_weight, tail_bias=tail_bias, cotangent=cotangent)


@jax.custom_vjp
def low(v):
    return lax.optimization_barrier(v.astype(jnp.bfloat16)).astype(jnp.float32)

@jax.custom_vjp
def low_back(v):
    return v

def low_keep(v):
    return (low(v), None)

def low_pass(kept, grad):
    return (grad,)

def back_keep(v):
    return (v, None)

def back_low(kept, grad):
    return (low(grad),)
low.defvjp(low_keep, low_pass)
low_back.defvjp(back_keep, back_low)
highest = lax.Precision.HIGHEST
eps = 1e-06

def matmul(left_side, right_side):
    return jnp.dot(left_side, right_side, precision=highest, preferred_element_type=jnp.float32)

def rescale(values):
    return values * lax.rsqrt(lax.optimization_barrier(jnp.mean(values * values, axis=1, keepdims=True)) + eps)

def aggregate(values, global_ids, shares):
    rows_per = NODE_DEV // 4
    blocks = global_ids.shape[0] // rows_per

    def one_block(pieces):
        node_ids, weights = pieces
        return lax.optimization_barrier(jnp.sum(weights[:, :, None] * values[node_ids], axis=1))
    blended = lax.map(jax.checkpoint(one_block), (global_ids.reshape(blocks, rows_per, K), shares.reshape(blocks, rows_per, K)))
    return blended.reshape(global_ids.shape[0], values.shape[1])

def forward(graph, params):
    global_ids, shares, is_board = graph
    pin_feats, board_feats, proj_weight, proj_bias, neigh_weight, neigh_bias, combine_weight, combine_bias, head_weight, head_bias, tail_weight, tail_bias = params
    board_act = jax.nn.gelu(low_back(matmul(board_feats, proj_weight) + proj_bias))
    hidden = low(jnp.where(is_board[:, None], board_act, pin_feats))
    for layer_idx in range(LAYERS):
        pre_neigh = low_back(matmul(hidden, neigh_weight[layer_idx]) + neigh_bias[layer_idx])
        shipped = low(jax.nn.gelu(pre_neigh))
        gathered = low(aggregate(shipped, global_ids, shares))
        pre_combine = low_back(matmul(hidden, combine_weight[layer_idx][:D]) + matmul(gathered, combine_weight[layer_idx][D:]) + combine_bias[layer_idx])
        hidden = low(rescale(jax.nn.gelu(pre_combine)))
    pre_head = low_back(matmul(hidden, head_weight) + head_bias)
    inner_act = low(jax.nn.gelu(pre_head))
    return matmul(inner_act, tail_weight) + tail_bias

def widen(array):
    return array.astype(jnp.float32)

def reference(pin_feats, board_feats, node_kinds, neighbours, visit_counts, pull_rows, proj_weight, proj_bias, neigh_weight, neigh_bias, combine_weight, combine_bias, head_weight, head_bias, tail_weight, tail_bias, cotangent):
    owners = (neighbours // CAP).astype(jnp.int32)
    targets = (jnp.arange(NODES, dtype=jnp.int32) // NODE_DEV)[:, None]
    global_ids = (owners * NODE_DEV + pull_rows[targets, neighbours]).astype(jnp.int32)
    counts = visit_counts.astype(jnp.float32)
    shares = counts / lax.optimization_barrier(jnp.sum(counts, axis=1, keepdims=True))
    is_board = node_kinds == 1
    params = (widen(pin_feats), widen(board_feats), widen(proj_weight), proj_bias, widen(neigh_weight), neigh_bias, widen(combine_weight), combine_bias, widen(head_weight), head_bias, widen(tail_weight), tail_bias)
    embeddings, pullback = jax.vjp(partial(forward, (global_ids, shares, is_board)), params)
    grads, = pullback(widen(cotangent))
    return (embeddings, grads[0], grads[1], grads[2], grads[3], grads[4], grads[5], grads[6], grads[7], grads[8], grads[9], grads[10], grads[11])
```

```python
import jax
import jax.numpy as jnp
from jax import lax
from jax.sharding import PartitionSpec as P

eps = 1e-06
bf16 = jnp.bfloat16
f32 = jnp.float32


def product(left_side, right_side):
    return jnp.dot(left_side, right_side, preferred_element_type=f32)


def product_t(left_side, right_side):
    return lax.dot_general(
        left_side, right_side, (((0,), (0,)), ((), ())), preferred_element_type=f32
    )


def product_rt(left_side, right_side):
    return lax.dot_general(
        left_side, right_side, (((1,), (1,)), ((), ())), preferred_element_type=f32
    )


def act_grad(pre_act, upstream):
    return jax.vjp(jax.nn.gelu, pre_act)[1](upstream)[0]


def swap(array, axis, distance):
    size = lax.axis_size(axis)
    return lax.ppermute(array, axis, [(i, i ^ distance) for i in range(size)])


def gather_cols(shard):
    size = lax.axis_size("cols")
    even = [shard] + [swap(shard, "cols", far) for far in range(2, size, 2)]
    blocks = []
    for block in even:
        blocks += [block, swap(block, "cols", 1)]
    return blocks


def natural(blocks):
    me = lax.axis_index("cols")
    step = 1
    while step < len(blocks):
        flip = (me & step) != 0
        blocks = [
            jnp.where(flip, blocks[j ^ step], blocks[j]) for j in range(len(blocks))
        ]
        step *= 2
    return blocks


def spread(shard):
    return jnp.concatenate(natural(gather_cols(shard)), axis=1)


def col_sum(partial_term):
    size = lax.axis_size("cols")
    blocks = natural(jnp.split(partial_term.astype(bf16), size, axis=1))
    total = blocks[0].astype(f32) + swap(blocks[1], "cols", 1).astype(f32)
    for far in range(2, size, 2):
        pair = blocks[far].astype(f32) + swap(blocks[far + 1], "cols", 1).astype(f32)
        total = total + swap(pair.astype(bf16), "cols", far).astype(f32)
    return total


def row_exchange(chunks, groups=None):
    return lax.all_to_all(
        chunks, "rows", split_axis=0, concat_axis=0, tiled=True, axis_index_groups=groups
    )


def chunked(terms):
    row_count = lax.axis_size("rows")
    return jnp.concatenate(
        [t.astype(bf16).reshape(row_count, -1, t.shape[-1]) for t in terms], axis=1
    )


def unchunked(kept, terms):
    row_count = lax.axis_size("rows")
    sizes = [t.shape[0] // row_count for t in terms]
    outs, at = [], 0
    for size in sizes:
        outs.append(kept[at : at + size])
        at += size
    return outs


def sum_rows_far(terms):
    kept = lax.psum_scatter(chunked(terms), "rows", scatter_dimension=0, tiled=True)
    return unchunked(kept[0].astype(f32), terms)


def sum_rows_near(terms):
    row_count = lax.axis_size("rows")
    chunks = chunked(terms)
    chunks = chunks.reshape((row_count // 2, 2) + chunks.shape[1:])
    odd = (lax.axis_index("rows") & 1) != 0
    mine = jnp.where(odd, chunks[:, 1], chunks[:, 0])
    other = jnp.where(odd, chunks[:, 0], chunks[:, 1])
    pair = (mine.astype(f32) + swap(other, "rows", 1).astype(f32)).astype(bf16)
    groups = [list(range(start, row_count, 2)) for start in range(2)]
    kept = jnp.sum(row_exchange(pair, groups).astype(f32), axis=0)
    return unchunked(kept, terms)


def sum_rows_last(terms, biases):
    row_count = lax.axis_size("rows")
    chunks = chunked(terms)
    stacked = jnp.concatenate(biases, axis=0)
    high_part = stacked.astype(bf16)
    low_part = (stacked - high_part.astype(f32)).astype(bf16)
    pad = (-2 * stacked.shape[0]) % 16
    tail = jnp.concatenate(
        [high_part, low_part, jnp.zeros((pad, stacked.shape[1]), bf16)], axis=0
    )
    tail = jnp.broadcast_to(tail[None], (row_count,) + tail.shape)
    kept = jnp.sum(
        row_exchange(jnp.concatenate([chunks, tail], axis=1)).astype(f32), axis=0
    )
    outs = unchunked(kept, terms)
    at = chunks.shape[1]
    count = stacked.shape[0]
    bias_sum = kept[at : at + count] + kept[at + count : at + 2 * count]
    return outs, bias_sum


def count_matrix(neighbours, visit_counts, pool_size):
    row_total, fan = neighbours.shape
    low_width = 128
    high_width = pool_size // low_width
    upper_idx = neighbours // low_width
    lower_idx = neighbours % low_width
    upper_hot = jnp.where(
        upper_idx[:, :, None] == jnp.arange(high_width, dtype=jnp.int32)[None, None, :],
        visit_counts[:, :, None],
        0,
    ).astype(bf16)
    lower_hot = (
        lower_idx[:, :, None] == jnp.arange(low_width, dtype=jnp.int32)[None, None, :]
    ).astype(bf16)
    dense = jnp.einsum("vkh,vkl->vhl", upper_hot, lower_hot, preferred_element_type=f32)
    return dense.astype(bf16).reshape(row_total, pool_size)


def row_scale(whole):
    wide = whole.astype(f32)
    return lax.rsqrt(jnp.sum(wide * wide, axis=1, keepdims=True) / whole.shape[1] + eps)


def body(
    pin_feats,
    board_feats,
    node_kinds,
    neighbours,
    visit_counts,
    pull_rows,
    proj_weight,
    proj_bias,
    neigh_weight,
    neigh_bias,
    combine_weight,
    combine_bias,
    head_weight,
    head_bias,
    tail_weight,
    tail_bias,
    cotangent,
):
    row_count = lax.axis_size("rows")
    capacity = pull_rows.shape[1] // row_count
    pool_size = pull_rows.shape[1]
    local_rows, channels = pin_feats.shape
    width = neigh_weight.shape[1]
    depth = neigh_weight.shape[0]
    is_board = (node_kinds == 1)[:, None]

    board_whole = spread(board_feats)
    board_pre = product(board_whole, proj_weight) + proj_bias
    hidden = jnp.where(is_board, jax.nn.gelu(board_pre), pin_feats.astype(f32)).astype(bf16)
    requested = row_exchange(pull_rows.reshape(row_count, capacity)).reshape(-1)
    selector = (
        requested[:, None] == jnp.arange(local_rows, dtype=jnp.int32)[None, :]
    ).astype(bf16)
    counts = count_matrix(neighbours, visit_counts, pool_size)
    inv_total = 1.0 / jnp.sum(visit_counts.astype(f32), axis=1, keepdims=True)

    kept = []
    act = hidden
    act_f32 = None
    scale = jnp.ones((local_rows, 1), f32)
    for l in range(depth):
        whole = spread(act)
        if l > 0:
            scale = row_scale(whole)
            kept[-1]["scale"] = scale
        neigh_raw = product(whole, neigh_weight[l])
        neigh_pre = scale * neigh_raw + neigh_bias[l]
        shipped = jax.nn.gelu(neigh_pre).astype(bf16)
        outgoing = product(selector, shipped).astype(bf16).reshape(-1, capacity, channels)
        pooled = row_exchange(outgoing).reshape(-1, channels)
        gathered = (product(counts, pooled) * inv_total).astype(bf16)
        gathered_whole = spread(gathered)
        self_raw = product(whole, combine_weight[l, :width])
        combine_pre = (
            scale * self_raw
            + product(gathered_whole, combine_weight[l, width:])
            + combine_bias[l]
        )
        act_f32 = jax.nn.gelu(combine_pre)
        act = act_f32.astype(bf16)
        kept.append(
            dict(
                whole=whole,
                in_scale=scale,
                neigh_raw=neigh_raw,
                neigh_pre=neigh_pre,
                self_raw=self_raw,
                combine_pre=combine_pre,
                gathered_whole=gathered_whole,
                act=act_f32,
            )
        )
    last_whole = spread(act)
    scale = row_scale(last_whole)
    kept[-1]["scale"] = scale
    head_raw = product(last_whole, head_weight)
    head_pre = scale * head_raw + head_bias
    inner_act = jax.nn.gelu(head_pre).astype(bf16)
    inner_grad = col_sum(product_rt(cotangent, tail_weight))
    head_grad = act_grad(head_pre, inner_grad).astype(bf16)
    head_wide = head_grad.astype(f32)
    upstream = col_sum(product_rt(head_grad, head_weight))
    dot = lax.psum(jnp.sum(head_raw * head_wide, axis=1, keepdims=True), "cols")
    inner_whole = spread(inner_act)
    embeddings = product(inner_whole, tail_weight) + tail_bias
    tail_bias_grad = jnp.sum(cotangent.astype(f32), axis=0, keepdims=True)
    head_bias_grad = jnp.sum(head_wide, axis=0, keepdims=True)
    tail_term = product_t(inner_whole, cotangent)
    head_term = product_t(last_whole, (scale * head_wide).astype(bf16))
    tail_out, head_out = sum_rows_far([tail_term, head_term])

    neigh_outs, combine_outs = [None] * depth, [None] * depth
    neigh_biases, combine_biases = [None] * depth, [None] * depth
    for l in reversed(range(depth)):
        saved = kept[l]
        scale = saved["scale"]
        in_scale = saved["in_scale"]
        act_upstream = scale * upstream - saved["act"] * (
            scale * scale * scale * dot / width
        )
        combine_grad = act_grad(saved["combine_pre"], act_upstream).astype(bf16)
        combine_wide = combine_grad.astype(f32)
        neigh_grad = col_sum(product_rt(combine_grad, combine_weight[l, width:]))
        pool_grad = product_t(counts, (neigh_grad * inv_total).astype(bf16))
        returned = row_exchange(
            pool_grad.astype(bf16).reshape(-1, capacity, channels)
        ).reshape(-1, channels)
        moved_grad = product_t(selector, returned)
        neigh_grad_pre = act_grad(saved["neigh_pre"], moved_grad).astype(bf16)
        neigh_wide = neigh_grad_pre.astype(f32)
        upstream = col_sum(
            product_rt(combine_grad, combine_weight[l, :width])
            + product_rt(neigh_grad_pre, neigh_weight[l])
        )
        if l > 0:
            dot = lax.psum(
                jnp.sum(
                    saved["self_raw"] * combine_wide + saved["neigh_raw"] * neigh_wide,
                    axis=1,
                    keepdims=True,
                ),
                "cols",
            )
        combine_biases[l] = jnp.sum(combine_wide, axis=0, keepdims=True)
        neigh_biases[l] = jnp.sum(neigh_wide, axis=0, keepdims=True)
        self_term = product_t(saved["whole"], (in_scale * combine_wide).astype(bf16))
        gathered_term = product_t(saved["gathered_whole"], combine_grad)
        neigh_term = product_t(saved["whole"], (in_scale * neigh_wide).astype(bf16))
        combine_term = jnp.concatenate([self_term, gathered_term], axis=0)
        reduce_rows = sum_rows_far if l > 0 else sum_rows_near
        combine_outs[l], neigh_outs[l] = reduce_rows([combine_term, neigh_term])

    grad_pin = jnp.where(is_board, 0.0, upstream)
    board_grad_pre = act_grad(board_pre, jnp.where(is_board, upstream, 0.0)).astype(bf16)
    proj_bias_grad = jnp.sum(board_grad_pre.astype(f32), axis=0, keepdims=True)
    grad_board = col_sum(product_rt(board_grad_pre, proj_weight))
    proj_term = product_t(board_whole, board_grad_pre)
    (proj_out,), biases = sum_rows_last(
        [proj_term],
        neigh_biases
        + combine_biases
        + [head_bias_grad, tail_bias_grad, proj_bias_grad],
    )
    return (
        embeddings,
        grad_pin,
        grad_board,
        proj_out,
        biases[2 * depth + 2],
        jnp.stack(neigh_outs),
        biases[:depth],
        jnp.stack(combine_outs),
        biases[depth : 2 * depth],
        head_out,
        biases[2 * depth],
        tail_out,
        biases[2 * depth + 1],
    )


def solution(mesh):
    placed = (
        P("rows", "cols"),
        P("rows", "cols"),
        P("rows"),
        P("rows", None),
        P("rows", None),
        P("rows", None),
        P(None, "cols"),
        P("cols"),
        P(None, None, "cols"),
        P(None, "cols"),
        P(None, None, "cols"),
        P(None, "cols"),
        P(None, "cols"),
        P("cols"),
        P(None, "cols"),
        P("cols"),
        P("rows", "cols"),
    )
    return jax.shard_map(
        body,
        mesh=mesh,
        in_specs=placed,
        out_specs=(
            P("rows", "cols"),
            P("rows", "cols"),
            P("rows", "cols"),
            P("rows", "cols"),
            P("cols"),
            P(None, "rows", "cols"),
            P(None, "cols"),
            P(None, "rows", "cols"),
            P(None, "cols"),
            P("rows", "cols"),
            P("cols"),
            P("rows", "cols"),
            P("cols"),
        ),
        check_vma=False,
    )
```

```python
import jax
import jax.numpy as jnp
from jax import lax
from jax.sharding import PartitionSpec as P

eps = 1e-06
bf16 = jnp.bfloat16
f32 = jnp.float32


def product(left_side, right_side):
    return jnp.dot(left_side, right_side, preferred_element_type=f32)


def product_t(left_side, right_side):
    return lax.dot_general(
        left_side, right_side, (((0,), (0,)), ((), ())), preferred_element_type=f32
    )


def product_rt(left_side, right_side):
    return lax.dot_general(
        left_side, right_side, (((1,), (1,)), ((), ())), preferred_element_type=f32
    )


def act_grad(pre_act, upstream):
    return jax.vjp(jax.nn.gelu, pre_act)[1](upstream)[0]


def swap(array, axis, distance):
    size = lax.axis_size(axis)
    return lax.ppermute(array, axis, [(i, i ^ distance) for i in range(size)])


def gather_cols(shard):
    size = lax.axis_size("cols")
    even = [shard] + [swap(shard, "cols", far) for far in range(2, size, 2)]
    blocks = []
    for block in even:
        blocks += [block, swap(block, "cols", 1)]
    return blocks


def natural(blocks):
    me = lax.axis_index("cols")
    step = 1
    while step < len(blocks):
        flip = (me & step) != 0
        blocks = [
            jnp.where(flip, blocks[j ^ step], blocks[j]) for j in range(len(blocks))
        ]
        step *= 2
    return blocks


def spread(shard):
    return jnp.concatenate(natural(gather_cols(shard)), axis=1)


def start_col_sum(partial_term):
    size = lax.axis_size("cols")
    blocks = natural(jnp.split(partial_term.astype(bf16), size, axis=1))
    near = (blocks[0], swap(blocks[1], "cols", 1))
    pairs = []
    for far in range(2, size, 2):
        pair = blocks[far].astype(f32) + swap(blocks[far + 1], "cols", 1).astype(f32)
        pairs.append(pair.astype(bf16))
    return near, pairs


def end_col_sum(near, pairs):
    total = near[0].astype(f32) + near[1].astype(f32)
    for far, pair in enumerate(pairs):
        total = total + swap(pair, "cols", 2 * far + 2).astype(f32)
    return total


def col_sum(partial_term):
    return end_col_sum(*start_col_sum(partial_term))


def vector_sum(values):
    step = 1
    while step < lax.axis_size("cols"):
        values = values + swap(values, "cols", step)
        step *= 2
    return values


def row_exchange(chunks, groups=None):
    return lax.all_to_all(
        chunks, "rows", split_axis=0, concat_axis=0, tiled=True, axis_index_groups=groups
    )


def chunked(terms):
    row_count = lax.axis_size("rows")
    return jnp.concatenate(
        [t.astype(bf16).reshape(row_count, -1, t.shape[-1]) for t in terms], axis=1
    )


def unchunked(kept, terms):
    row_count = lax.axis_size("rows")
    sizes = [t.shape[0] // row_count for t in terms]
    outs, at = [], 0
    for size in sizes:
        outs.append(kept[at : at + size])
        at += size
    return outs


def halve(chunks, distance):
    chunks = chunks.reshape((chunks.shape[0] // 2, 2) + chunks.shape[1:])
    bit = jnp.where((lax.axis_index("rows") & distance) != 0, 1, 0)
    keep = lax.dynamic_index_in_dim(chunks, bit, 1, keepdims=False)
    send = lax.dynamic_index_in_dim(chunks, 1 - bit, 1, keepdims=False)
    return (keep.astype(f32) + swap(send, "rows", distance).astype(f32)).astype(bf16)


def finish(chunks, terms):
    distance = lax.axis_size("rows") // chunks.shape[0]
    while chunks.shape[0] > 1:
        chunks = halve(chunks, distance)
        distance *= 2
    return unchunked(chunks[0].astype(f32), terms)


def tie(*arrays):
    return lax.optimization_barrier(arrays)


def sum_rows_last(terms, biases):
    row_count = lax.axis_size("rows")
    chunks = chunked(terms)
    stacked = jnp.concatenate(biases, axis=0)
    high_part = stacked.astype(bf16)
    low_part = (stacked - high_part.astype(f32)).astype(bf16)
    pad = (-2 * stacked.shape[0]) % 16
    tail = jnp.concatenate(
        [high_part, low_part, jnp.zeros((pad, stacked.shape[1]), bf16)], axis=0
    )
    tail = jnp.broadcast_to(tail[None], (row_count,) + tail.shape)
    kept = jnp.sum(
        row_exchange(jnp.concatenate([chunks, tail], axis=1)).astype(f32), axis=0
    )
    outs = unchunked(kept, terms)
    at = chunks.shape[1]
    count = stacked.shape[0]
    bias_sum = kept[at : at + count] + kept[at + count : at + 2 * count]
    return outs, bias_sum


def count_matrix(neighbours, visit_counts, pool_size):
    row_total, fan = neighbours.shape
    low_width = 128
    high_width = pool_size // low_width
    upper_idx = neighbours // low_width
    lower_idx = neighbours % low_width
    upper_hot = jnp.where(
        upper_idx[:, :, None] == jnp.arange(high_width, dtype=jnp.int32)[None, None, :],
        visit_counts[:, :, None],
        0,
    ).astype(bf16)
    lower_hot = (
        lower_idx[:, :, None] == jnp.arange(low_width, dtype=jnp.int32)[None, None, :]
    ).astype(bf16)
    dense = jnp.einsum("vkh,vkl->vhl", upper_hot, lower_hot, preferred_element_type=f32)
    return dense.astype(bf16).reshape(row_total, pool_size)


def row_scale(whole):
    wide = whole.astype(f32)
    return lax.rsqrt(jnp.sum(wide * wide, axis=1, keepdims=True) / whole.shape[1] + eps)


def body(
    pin_feats,
    board_feats,
    node_kinds,
    neighbours,
    visit_counts,
    pull_rows,
    proj_weight,
    proj_bias,
    neigh_weight,
    neigh_bias,
    combine_weight,
    combine_bias,
    head_weight,
    head_bias,
    tail_weight,
    tail_bias,
    cotangent,
):
    row_count = lax.axis_size("rows")
    capacity = pull_rows.shape[1] // row_count
    pool_size = pull_rows.shape[1]
    local_rows, channels = pin_feats.shape
    width = neigh_weight.shape[1]
    depth = neigh_weight.shape[0]
    is_board = (node_kinds == 1)[:, None]

    board_whole = spread(board_feats)
    board_pre = product(board_whole, proj_weight) + proj_bias
    hidden = jnp.where(is_board, jax.nn.gelu(board_pre), pin_feats.astype(f32)).astype(bf16)
    requested = row_exchange(pull_rows.reshape(row_count, capacity)).reshape(-1)
    selector = (
        requested[:, None] == jnp.arange(local_rows, dtype=jnp.int32)[None, :]
    ).astype(bf16)
    inv_total = 1.0 / jnp.sum(visit_counts.astype(f32), axis=1, keepdims=True)

    hidden, selector, inv_total = tie(hidden, selector, inv_total)
    inner_grad = None

    kept = []
    act = hidden
    scale = jnp.ones((local_rows, 1), f32)
    for l in range(depth):
        whole = spread(act)
        if l > 0:
            scale = row_scale(whole)
            kept[-1]["scale"] = scale
        neigh_raw = product(whole, neigh_weight[l])
        neigh_pre = scale * neigh_raw + neigh_bias[l]
        shipped = jax.nn.gelu(neigh_pre).astype(bf16)
        outgoing = product(selector, shipped).astype(bf16).reshape(-1, capacity, channels)
        pooled = row_exchange(outgoing).reshape(-1, channels)
        whole_late, cotangent_late, _ = tie(whole, cotangent, outgoing)
        self_raw = product(whole_late, combine_weight[l, :width])
        if l == 0:
            inner_grad = col_sum(product_rt(cotangent_late, tail_weight))
            counts = count_matrix(neighbours, visit_counts, pool_size)
            counts, inner_grad, pooled, self_raw = tie(counts, inner_grad, pooled, self_raw)
        else:
            pooled, self_raw = tie(pooled, self_raw)
        gathered = (product(counts, pooled) * inv_total).astype(bf16)
        gathered_whole = spread(gathered)
        combine_pre = (
            scale * self_raw
            + product(gathered_whole, combine_weight[l, width:])
            + combine_bias[l]
        )
        act_f32 = jax.nn.gelu(combine_pre)
        act = act_f32.astype(bf16)
        kept.append(
            dict(
                whole=whole,
                in_scale=scale,
                neigh_raw=neigh_raw,
                neigh_pre=neigh_pre,
                self_raw=self_raw,
                combine_pre=combine_pre,
                gathered_whole=gathered_whole,
                act=act_f32,
            )
        )
    last_whole = spread(act)
    scale = row_scale(last_whole)
    kept[-1]["scale"] = scale
    head_raw = product(last_whole, head_weight)
    head_pre = scale * head_raw + head_bias
    inner_act = jax.nn.gelu(head_pre).astype(bf16)
    head_grad = act_grad(head_pre, inner_grad).astype(bf16)
    head_wide = head_grad.astype(f32)
    near, pairs = start_col_sum(product_rt(head_grad, head_weight))
    dot = vector_sum(jnp.sum(head_raw * head_wide, axis=1))
    dot = dot[:, None]
    head_late, last_late, _ = tie(head_wide, last_whole, pairs[0])
    head_term = product_t(last_late, (scale * head_late).astype(bf16))
    head_bias_grad = jnp.sum(head_late, axis=0, keepdims=True)
    head_sum = halve(chunked([head_term]), 1)
    upstream = end_col_sum(near, pairs)

    neigh_outs, combine_outs = [None] * depth, [None] * depth
    neigh_biases, combine_biases = [None] * depth, [None] * depth
    early = [head_sum]
    for l in reversed(range(depth)):
        saved = kept[l]
        scale = saved["scale"]
        in_scale = saved["in_scale"]
        act_upstream = scale * upstream - saved["act"] * (
            scale * scale * scale * dot / width
        )
        combine_grad = act_grad(saved["combine_pre"], act_upstream).astype(bf16)
        near, pairs = start_col_sum(product_rt(combine_grad, combine_weight[l, width:]))
        if l < depth - 1:
            first, second, _ = tie(early[0], early[1], pairs[0])
            early = [halve(first, 2), halve(second, 4)]
        neigh_grad = end_col_sum(near, pairs)
        pool_grad = product_t(counts, (neigh_grad * inv_total).astype(bf16))
        pool_grad = pool_grad.astype(bf16).reshape(-1, capacity, channels)
        pool_grad, *early = tie(pool_grad, *early)
        returned = row_exchange(pool_grad).reshape(-1, channels)

        combine_grad, inner_act, _ = tie(combine_grad, inner_act, pool_grad)
        combine_wide = combine_grad.astype(f32)
        self_grad = product_rt(combine_grad, combine_weight[l, :width])
        combine_biases[l] = jnp.sum(combine_wide, axis=0, keepdims=True)
        self_term = product_t(saved["whole"], (in_scale * combine_wide).astype(bf16))
        gathered_term = product_t(saved["gathered_whole"], combine_grad)
        combine_term = jnp.concatenate([self_term, gathered_term], axis=0)
        combine_sum = halve(chunked([combine_term]), 1)
        if l == depth - 1:
            inner_whole = spread(inner_act)
            embeddings = product(inner_whole, tail_weight) + tail_bias
            tail_bias_grad = jnp.sum(cotangent.astype(f32), axis=0, keepdims=True)
            tail_term = product_t(inner_whole, cotangent)
            (head_out,) = finish(early[0], [head_term])
            returned, combine_sum, self_grad, tail_term, head_out = tie(
                returned, combine_sum, self_grad, tail_term, head_out
            )
        else:
            returned, combine_sum, self_grad = tie(returned, combine_sum, self_grad)

        moved_grad = product_t(selector, returned)
        neigh_grad_pre = act_grad(saved["neigh_pre"], moved_grad).astype(bf16)
        neigh_wide = neigh_grad_pre.astype(f32)
        near, pairs = start_col_sum(self_grad + product_rt(neigh_grad_pre, neigh_weight[l]))
        if l > 0:
            dot = vector_sum(
                jnp.sum(
                    saved["self_raw"] * combine_wide + saved["neigh_raw"] * neigh_wide,
                    axis=1,
                )
            )
            dot = dot[:, None]
        neigh_late, combine_sum, _ = tie(neigh_wide, combine_sum, pairs[0])
        neigh_biases[l] = jnp.sum(neigh_late, axis=0, keepdims=True)
        neigh_term = product_t(saved["whole"], (in_scale * neigh_late).astype(bf16))
        if l == depth - 1:
            terms = [tail_term, neigh_term]
            terms_sum = halve(chunked(terms), 1)
            early = [terms_sum, halve(combine_sum, 2)]
            upstream, *early = tie(end_col_sum(near, pairs), *early)
            last_combine = combine_term
        else:
            terms_sum = halve(chunked([neigh_term]), 1)
            combine_sum = halve(combine_sum, 2)
            upstream, terms_sum, combine_sum = tie(
                end_col_sum(near, pairs), terms_sum, combine_sum
            )

    grad_pin = jnp.where(is_board, 0.0, upstream)
    board_grad_pre = act_grad(board_pre, jnp.where(is_board, upstream, 0.0)).astype(bf16)
    proj_bias_grad = jnp.sum(board_grad_pre.astype(f32), axis=0, keepdims=True)
    grad_board = col_sum(product_rt(board_grad_pre, proj_weight))
    proj_term = product_t(board_whole, board_grad_pre)
    (proj_out,), biases = sum_rows_last(
        [proj_term],
        neigh_biases
        + combine_biases
        + [head_bias_grad, tail_bias_grad, proj_bias_grad],
    )
    tail_out, neigh_outs[1] = finish(early[0], [tail_term, neigh_term])
    (combine_outs[1],) = finish(early[1], [last_combine])
    (combine_outs[0],) = finish(combine_sum, [combine_term])
    (neigh_outs[0],) = finish(terms_sum, [neigh_term])
    return (
        embeddings,
        grad_pin,
        grad_board,
        proj_out,
        biases[2 * depth + 2],
        jnp.stack(neigh_outs),
        biases[:depth],
        jnp.stack(combine_outs),
        biases[depth : 2 * depth],
        head_out,
        biases[2 * depth],
        tail_out,
        biases[2 * depth + 1],
    )


def solution(mesh):
    placed = (
        P("rows", "cols"),
        P("rows", "cols"),
        P("rows"),
        P("rows", None),
        P("rows", None),
        P("rows", None),
        P(None, "cols"),
        P("cols"),
        P(None, None, "cols"),
        P(None, "cols"),
        P(None, None, "cols"),
        P(None, "cols"),
        P(None, "cols"),
        P("cols"),
        P(None, "cols"),
        P("cols"),
        P("rows", "cols"),
    )
    return jax.shard_map(
        body,
        mesh=mesh,
        in_specs=placed,
        out_specs=(
            P("rows", "cols"),
            P("rows", "cols"),
            P("rows", "cols"),
            P("rows", "cols"),
            P("cols"),
            P(None, "rows", "cols"),
            P(None, "cols"),
            P(None, "rows", "cols"),
            P(None, "cols"),
            P("rows", "cols"),
            P("cols"),
            P("rows", "cols"),
            P("cols"),
        ),
        check_vma=False,
    )
```

```python
import jax
import jax.numpy as jnp
from jax import lax
from jax.experimental import pallas as pl
from jax.experimental.pallas import tpu as pltpu
from jax.sharding import PartitionSpec as P

eps = 1e-06
bf16 = jnp.bfloat16
f32 = jnp.float32
MIB = 1 << 20
PLACE = {}


def tie(*arrays):
    return lax.optimization_barrier(arrays)


def gate(arrays, *tokens):
    return list(tie(*arrays, *tokens)[: len(arrays)])


def product(left_side, right_side):
    return jnp.dot(left_side, right_side, preferred_element_type=f32)


def product_t(left_side, right_side):
    return lax.dot_general(
        left_side, right_side, (((0,), (0,)), ((), ())), preferred_element_type=f32
    )


def product_rt(left_side, right_side):
    return lax.dot_general(
        left_side, right_side, (((1,), (1,)), ((), ())), preferred_element_type=f32
    )


def tanh_of(x):
    return jnp.tanh(0.7978845608028654 * (x + 0.044715 * (x * x * x)))


def gelu(x):
    return 0.5 * x * (1.0 + tanh_of(x))


def gelu_grad(x):
    t = tanh_of(x)
    slope = 0.7978845608028654 * (1.0 + 0.134145 * (x * x))
    return 0.5 * (1.0 + t) + 0.5 * x * (1.0 - t * t) * slope


def swap(array, axis, distance):
    size = lax.axis_size(axis)
    return lax.ppermute(array, axis, [(i, i ^ distance) for i in range(size)])


def gather_cols(shard, beside=()):
    size = lax.axis_size("cols")
    far = [swap(shard, "cols", step) for step in range(2, size, 2)]
    if beside:
        tied = tie(*far, *beside)
        far, beside = tied[: len(far)], tied[len(far) :]
    blocks = []
    for block in [shard, *far]:
        blocks += [block, swap(block, "cols", 1)]
    return (blocks, beside) if beside else blocks


def pair_sums(blocks, dot=None):
    evens, odds = blocks[2::2], blocks[3::2]
    came = [swap(odd, "cols", 1) for odd in odds]
    near = [blocks[0], swap(blocks[1], "cols", 1)]
    outs = [(block.shape, bf16) for block in evens]
    if dot is None:
        return near, list(call(pair_kernel, outs, *evens, *came))
    *pairs, dot = call(
        pair_dot_kernel, outs + [(dot.shape, f32)], *evens, *came, dot, swap(dot, "cols", 1)
    )
    return near, pairs, dot


def parts_of(near, pairs, beside=()):
    far = [swap(pair, "cols", 2 * i + 2) for i, pair in enumerate(pairs)]
    parts = tie(*near, *far, *beside)
    count = 2 + len(far)
    return (parts[:count], parts[count:]) if beside else parts


def all_chips(dot):
    return [dot] + [
        swap(dot, "cols", far) for far in range(2, lax.axis_size("cols"), 2)
    ]


def row_exchange(chunks):
    return lax.all_to_all(chunks, "rows", split_axis=0, concat_axis=0, tiled=True)


def row_order():
    return list(reversed(range(lax.axis_size("rows"))))


def exchange(chunks):
    return [
        swap(chunk, "rows", k) if k else chunk for k, chunk in zip(row_order(), chunks)
    ]


class Going:
    def __init__(self, pieces, keep, send, level):
        self.pieces, self.keep, self.level = pieces, keep, level
        self.came = swap(send, "rows", 1 << level)

    def after(self, token):
        self.keep, self.came = gate([self.keep, self.came], token)
        return self


VECTORS = (0, 16)


def halves(pieces):
    return [(n // 2, m) for n, m in pieces]


def rows_of(pieces):
    return sum(n * m if n else m for n, m in pieces)


def fold(*goings):
    pieces = [p for going in goings for p in going.pieces]
    level = goings[0].level + 1
    half = halves(pieces)
    shape = (rows_of(half), goings[0].keep.shape[1])
    arrays = [a for going in goings for a in (going.keep, going.came)]
    kernel = form(fold_kernel, [going.pieces for going in goings], level)
    keep, send = call(kernel, [(shape, bf16)] * 2, *arrays)
    return Going(half, keep, send, level)


def close(going):
    while going.pieces[0][0] > 1:
        going = fold(going)
    total = going.keep.astype(f32) + going.came.astype(f32)
    outs, at = [], 0
    for n, m in going.pieces:
        part = total[at : at + m]
        outs.append(part if n else part[: m // 2] + part[m // 2 :])
        at += m
    return outs


def form(kernel, *options):
    def run(*refs):
        kernel(*options, *refs)

    run.__name__ = kernel.__name__
    return run


def call(kernel, outs, *ins, saved=(), scratch=(), flops=0):
    vmem = pl.BlockSpec(memory_space=pltpu.VMEM)
    shapes = [jax.ShapeDtypeStruct(shape, dtype) for shape, dtype in outs]
    placed = [pltpu.HBM(shape, dtype) for shape, dtype in saved]
    size = sum(a.size * a.dtype.itemsize for a in ins)
    size += sum(jnp.dtype(t).itemsize * n[0] * n[1] for n, t in list(outs) + list(saved))
    extra = sum(jnp.dtype(t).itemsize * n[0] * n[1] for n, t in saved)

    def run(me_ref, *refs):
        if not saved:
            kernel(me_ref, *refs)
            return
        inner = len(ins) + len(outs)
        count = len(saved)
        targets, held = refs[inner : inner + count], refs[inner + count : -1]
        kernel(me_ref, *refs[:inner], *held)
        copies = [
            pltpu.make_async_copy(held[i], targets[i], refs[-1].at[i])
            for i in range(count)
        ]
        for copy in copies:
            copy.start()
        for copy in copies:
            copy.wait()

    return pl.pallas_call(
        run,
        out_shape=shapes + placed,
        in_specs=[pl.BlockSpec(memory_space=pltpu.SMEM)] + [vmem] * len(ins),
        out_specs=[vmem] * len(shapes)
        + [pl.BlockSpec(memory_space=pltpu.HBM)] * len(placed),
        scratch_shapes=[pltpu.VMEM(shape, dtype) for shape, dtype in [*saved, *scratch]]
        + ([pltpu.SemaphoreType.DMA((len(saved),))] if saved else []),
        cost_estimate=pl.CostEstimate(flops=flops, bytes_accessed=size, transcendentals=0),
        compiler_params=pltpu.CompilerParams(
            vmem_limit_bytes=max(12 * MIB, size * 5 // 4 + extra + 6 * MIB)
        ),
        name=kernel.__name__,
    )(PLACE["me"], *ins)


def copy_in(*parts):
    arrays = [part[0] for part in parts]
    count = len(parts)
    shapes = []
    for array, index, rows in parts:
        size = array.shape[-2] if rows is None else rows[1] - rows[0]
        shapes.append(jax.ShapeDtypeStruct((size, array.shape[-1]), array.dtype))

    def run(*refs):
        sems = refs[-1]
        copies = []
        for i, (array, index, rows) in enumerate(parts):
            source = refs[i] if index is None else refs[i].at[index]
            if rows is not None:
                source = source.at[pl.ds(rows[0], rows[1] - rows[0])]
            copies.append(pltpu.make_async_copy(source, refs[count + i], sems.at[i]))
        for copy in copies:
            copy.start()
        for copy in copies:
            copy.wait()

    size = sum(s.size * s.dtype.itemsize for s in shapes)
    return pl.pallas_call(
        run,
        out_shape=shapes,
        in_specs=[pl.BlockSpec(memory_space=pltpu.HBM)] * count,
        out_specs=[pl.BlockSpec(memory_space=pltpu.VMEM)] * count,
        scratch_shapes=[pltpu.SemaphoreType.DMA((count,))],
        cost_estimate=pl.CostEstimate(flops=0, bytes_accessed=size, transcendentals=0),
        compiler_params=pltpu.CompilerParams(vmem_limit_bytes=size * 2 + 4 * MIB),
    )(*[pltpu.with_memory_space_constraint(a, pltpu.HBM) for a in arrays])


def block_rows(me_ref, j, size):
    return pl.ds(pl.multiple_of((me_ref[0] ^ j) * size, size), size)


def sum_refs(refs):
    total = refs[0][...].astype(f32)
    for ref in refs[1:]:
        total = total + ref[...].astype(f32)
    return total


def blocks_product(me_ref, block_refs, weight_ref):
    total = None
    for j, ref in enumerate(block_refs):
        rows = block_rows(me_ref, j, ref.shape[1])
        term = product(ref[...], weight_ref[rows, :])
        total = term if total is None else total + term
    return total


def blocks_scale(block_refs):
    total = None
    for ref in block_refs:
        wide = ref[...].astype(f32)
        term = jnp.sum(wide * wide, axis=1, keepdims=True)
        total = term if total is None else total + term
    return lax.rsqrt(total / (len(block_refs) * block_refs[0].shape[1]) + eps)


def lane_mask():
    return lax.broadcasted_iota(jnp.int32, (128, 128), 0) == lax.broadcasted_iota(
        jnp.int32, (128, 128), 1
    )


def to_lanes(column, out_ref):
    mask = lane_mask()
    for i in range(out_ref.shape[0]):
        part = jnp.where(mask, column[i * 128 : (i + 1) * 128], 0.0)
        out_ref[i : i + 1, :] = jnp.sum(part, axis=0, keepdims=True)


def from_lanes(rows):
    mask = lane_mask()
    return jnp.concatenate(
        [
            jnp.sum(jnp.where(mask, rows[i : i + 1, :], 0.0), axis=1, keepdims=True)
            for i in range(rows.shape[0])
        ],
        axis=0,
    )


def pair_kernel(me_ref, *refs):
    count = len(refs) // 3
    for one, other, out in zip(refs[:count], refs[count : 2 * count], refs[2 * count :]):
        out[...] = (one[...].astype(f32) + other[...].astype(f32)).astype(bf16)


def pair_dot_kernel(me_ref, *refs):
    count = (len(refs) - 3) // 3
    blocks, rest = refs[: 2 * count], refs[2 * count :]
    pair_kernel(me_ref, *blocks, *rest[2 : 2 + count])
    rest[-1][...] = rest[0][...] + rest[1][...]


def flat_kernel(me_ref, dense, out):
    nodes = out.shape[0]
    groups = dense.shape[0] // nodes
    for h in range(groups):
        part = dense[pl.ds(h, nodes, stride=groups), :]
        out[:, h * 128 : (h + 1) * 128] = part.astype(bf16)


def counts_kernel(me_ref, own, other, out, out_t):
    core = me_ref[0] & 1
    size = own.shape[0]
    for ref, place in ((own, core), (other, 1 - core)):
        rows = pl.ds(pl.multiple_of(place * size, size), size)
        value = ref[...]
        out[rows, :] = value
        out_t[:, rows] = value.T


def board_kernel(count, save, me_ref, *refs):
    blocks, refs = refs[:count], refs[count:]
    weight, bias, *refs = refs
    pre = blocks_product(me_ref, blocks, weight) + bias[...]
    if save:
        refs[0][...] = pre
        return
    pin, kinds, hidden_out = refs
    board = from_lanes(kinds) > 0.5
    hidden_out[...] = jnp.where(board, gelu(pre), pin[...].astype(f32)).astype(bf16)


def chunk_span(me_ref, k, size):
    return pl.ds(pl.multiple_of((me_ref[1] ^ k) * size, size), size)


def send_chunks(me_ref, matrix, value, outs, first):
    for i, out in enumerate(outs):
        rows = chunk_span(me_ref, first - i, out.shape[0])
        out[...] = product(matrix[rows, :], value).astype(bf16)


def rest_kernel(me_ref, value, matrix, *outs):
    send_chunks(me_ref, matrix, value[...], outs, len(outs) - 1)


def take_chunks(me_ref, matrix, chunks):
    total = None
    for k, ref in zip(reversed(range(len(chunks))), chunks):
        term = product(matrix[:, chunk_span(me_ref, k, ref.shape[0])], ref[...])
        total = term if total is None else total + term
    return total


def neigh_kernel(count, scaled, me_ref, *refs):
    blocks, refs = refs[:count], refs[count:]
    weight, bias, selector, moved_out, *outs = refs
    pre = blocks_product(me_ref, blocks, weight)
    if scaled:
        pre = blocks_scale(blocks) * pre
    moved = gelu(pre + bias[...]).astype(bf16)
    moved_out[...] = moved
    send_chunks(me_ref, selector, moved, outs, 2 * len(outs) - 1)


def neigh_save_kernel(count, scaled, me_ref, *refs):
    blocks, refs = refs[:count], refs[count:]
    weight, bias, self_w, self_out, pre_out, *refs = refs
    raw = blocks_product(me_ref, blocks, weight)
    if scaled:
        scale_out, raw_out = refs
        scale = blocks_scale(blocks)
        to_lanes(scale, scale_out)
        raw_out[...] = raw
        pre_out[...] = scale * raw + bias[...]
    else:
        pre_out[...] = raw + bias[...]
    self_out[...] = blocks_product(me_ref, blocks, self_w)


def aggregate_kernel(count, me_ref, *refs):
    chunks, (counts, inv_total, out) = refs[:count], refs[count:]
    total = take_chunks(me_ref, counts, chunks)
    out[...] = (total * from_lanes(inv_total)).astype(bf16)


def combine_kernel(count, scaled, save, me_ref, *refs):
    blocks, refs = refs[:count], refs[count:]
    weight, bias, self_raw, *refs = refs
    pre = blocks_product(me_ref, blocks, weight)
    own = self_raw[...]
    if scaled:
        own = from_lanes(refs[0]) * own
    pre = own + pre + bias[...]
    if save:
        refs[-1][...] = pre
    else:
        refs[-1][...] = gelu(pre).astype(bf16)


def blocks_rt(me_ref, pairs, outs):
    for j in reversed(range(len(outs))):
        rows = block_rows(me_ref, j, outs[j].shape[1])
        total = None
        for g, w in pairs:
            term = product_rt(g, w[rows, :])
            total = term if total is None else total + term
        outs[j][...] = total.astype(bf16)


def rt_kernel(me_ref, grad, weight, *outs):
    blocks_rt(me_ref, [(grad[...], weight)], outs)


def head_kernel(count, me_ref, *refs):
    blocks, refs = refs[:count], refs[count:]
    parts, refs = refs[: count // 2 + 1], refs[count // 2 + 1 :]
    weight, bias, *outs = refs
    outs, (dot_out, grad_out, scale_out, inner_out) = outs[:count], outs[count:]
    raw = blocks_product(me_ref, blocks, weight)
    scale = blocks_scale(blocks)
    to_lanes(scale, scale_out)
    pre = scale * raw + bias[...]
    inner_out[...] = gelu(pre).astype(bf16)
    grad = (sum_refs(parts) * gelu_grad(pre)).astype(bf16)
    grad_out[...] = grad
    blocks_rt(me_ref, [(grad, weight)], outs)
    to_lanes(jnp.sum(raw * grad.astype(f32), axis=1, keepdims=True), dot_out)


def combine_back_kernel(count, width, me_ref, *refs):
    parts, refs = refs[: count // 2 + 1], refs[count // 2 + 1 :]
    dots, refs = refs[: count // 2], refs[count // 2 :]
    weight, scale, pre, *outs, grad_out = refs
    dot = sum_refs(dots)
    scale, pre = from_lanes(scale), pre[...]
    factor = scale * scale * scale * from_lanes(dot) / width
    act_grad = scale * sum_refs(parts) - gelu(pre) * factor
    grad = (act_grad * gelu_grad(pre)).astype(bf16)
    grad_out[...] = grad
    blocks_rt(me_ref, [(grad, weight)], outs)


def pool_back_kernel(count, me_ref, *refs):
    parts, refs = refs[: count // 2 + 1], refs[count // 2 + 1 :]
    counts_t, inv_total, grad_out, *outs = refs
    grad = (sum_refs(parts) * from_lanes(inv_total)).astype(bf16)
    grad_out[...] = grad
    send_chunks(me_ref, counts_t, grad, outs, 2 * len(outs) - 1)


def neigh_back_kernel(count, cols, dotted, me_ref, *refs):
    chunks, refs = refs[:count], refs[count:]
    select_t, pre, combine_grad, self_w, weight, *refs = refs
    grad = (take_chunks(me_ref, select_t, chunks) * gelu_grad(pre[...])).astype(bf16)
    own = combine_grad[...]
    if dotted:
        self_raw, raw, *refs = refs
        dot = self_raw[...] * own.astype(f32) + raw[...] * grad.astype(f32)
        to_lanes(jnp.sum(dot, axis=1, keepdims=True), refs[-1])
    refs[cols][...] = grad
    blocks_rt(me_ref, [(own, self_w), (grad, weight)], refs[:cols])


def board_back_kernel(count, row_count, me_ref, *refs):
    parts, refs = refs[: count // 2 + 1], refs[count // 2 + 1 :]
    blocks, refs = refs[:count], refs[count:]
    pre, kinds, weight, *refs = refs
    biases, refs = refs[:6], refs[6:]
    outs, (keep, send, sums, pin_out) = refs[:count], refs[count:]
    total = sum_refs(parts)
    board = from_lanes(kinds) > 0.5
    wide = jnp.where(board, total, 0.0) * gelu_grad(pre[...])
    grad = wide.astype(bf16)
    rows = keep.shape[0] - 16
    terms_kernel(
        [(count, False)],
        row_count,
        me_ref,
        *blocks,
        grad,
        keep.at[pl.ds(0, rows)],
        send.at[pl.ds(0, rows)],
        sums,
    )
    last = sums[...]
    stacked = [ref[...] for ref in biases] + [last, jnp.zeros_like(last)]
    stacked = split_vectors(jnp.concatenate(stacked, axis=0))
    keep[rows : rows + 16, :] = stacked
    send[rows : rows + 16, :] = stacked
    blocks_rt(me_ref, [(grad, weight)], outs)
    pin_out[...] = jnp.where(board, 0.0, total)


def place_piece(stay, keep, send, at, value):
    rows = pl.ds(pl.multiple_of(at, 16), value.shape[0])

    @pl.when(stay)
    def _():
        keep[rows, :] = value

    @pl.when(jnp.logical_not(stay))
    def _():
        send[rows, :] = value


def terms_kernel(sets, row_count, me_ref, *refs):
    *refs, keep, send, sum_out = refs
    count = sum(n for n, _ in sets)
    blocks, refs = refs[:count], refs[count:]
    grad = refs[0][...]
    wide = grad.astype(f32)
    sum_out[...] = jnp.sum(wide, axis=0, keepdims=True)
    total = sum(ref.shape[1] for ref in blocks)
    chunk = total // row_count
    bit = me_ref[1] & 1
    base = 0
    for n, scaled in sets:
        value = (from_lanes(refs[1]) * wide).astype(bf16) if scaled else grad
        for j in range(n):
            ref = blocks[j]
            size = ref.shape[1]
            part = product_t(ref[...], value).astype(bf16)
            step = min(size, chunk)
            first = base + (me_ref[0] ^ j) * size
            for i in range(size // step):
                start = first + i * step
                q = start // chunk
                at = (q // 2) * chunk + start % chunk
                stay = (q & 1) == bit
                place_piece(stay, keep, send, at, part[i * step : (i + 1) * step])
        base += sum(ref.shape[1] for ref in blocks[:n])
        blocks = blocks[n:]


def both_kernel(count, other_count, row_count, me_ref, *refs):
    first, refs = refs[: count + 1], refs[count + 1 :]
    second, (keep, send, sums, other_sums) = refs[: other_count + 2], refs[other_count + 2 :]
    rows = sum(ref.shape[1] for ref in first[:count]) // 2
    rest = keep.shape[0] - rows
    terms_kernel(
        [(count, False)], row_count, me_ref, *first, keep.at[pl.ds(0, rows)], send.at[pl.ds(0, rows)], sums
    )
    terms_kernel(
        [(other_count, True)],
        row_count,
        me_ref,
        *second,
        keep.at[pl.ds(rows, rest)],
        send.at[pl.ds(rows, rest)],
        other_sums,
    )


def tail_kernel(count, row_count, me_ref, *refs):
    blocks, refs = refs[:count], refs[count:]
    weight, bias, cotangent, keep, send, sum_out, out = refs
    out[...] = blocks_product(me_ref, blocks, weight) + bias[...]
    terms_kernel(
        [(count, False)], row_count, me_ref, *blocks, cotangent, keep, send, sum_out
    )


def split_vectors(values):
    high = values.astype(bf16).astype(f32)
    return jnp.concatenate([high, values - high], axis=0).astype(bf16)


def fold_kernel(groups, level, me_ref, *refs):
    *refs, keep, send = refs
    bit = (me_ref[1] >> level) & 1
    base = 0
    for i, pieces in enumerate(groups):
        one, other = refs[2 * i], refs[2 * i + 1]
        at = 0
        for n, m in pieces:
            if n == 0:
                span = slice(at, at + m)
                total = one[span, :].astype(f32) + other[span, :].astype(f32)
                total = split_vectors(total[: m // 2] + total[m // 2 :])
                keep[base : base + m, :] = total
                send[base : base + m, :] = total
                at += m
                base += m
            for q in range(0, n, 2):
                rows = slice(base + (q // 2) * m, base + (q // 2 + 1) * m)
                for out, place in ((keep, bit), (send, 1 - bit)):
                    span = pl.ds(pl.multiple_of(at + (q + place) * m, 16), m)
                    total = one[span, :].astype(f32) + other[span, :].astype(f32)
                    out[rows, :] = total.astype(bf16)
            at += n * m
            base += (n // 2) * m


def dense_counts(neighbours, visit_counts, pool_size):
    low_width = 128
    high_width = pool_size // low_width
    upper_idx = neighbours // low_width
    lower_idx = neighbours % low_width
    upper_hot = jnp.where(
        upper_idx[:, :, None] == jnp.arange(high_width, dtype=jnp.int32)[None, None, :],
        visit_counts[:, :, None],
        0,
    ).astype(bf16)
    lower_hot = (
        lower_idx[:, :, None] == jnp.arange(low_width, dtype=jnp.int32)[None, None, :]
    ).astype(bf16)
    dense = jnp.einsum("vkh,vkl->vhl", upper_hot, lower_hot, preferred_element_type=f32)
    return dense.reshape(-1, low_width)


def body(
    pin_feats,
    board_feats,
    node_kinds,
    neighbours,
    visit_counts,
    pull_rows,
    proj_weight,
    proj_bias,
    neigh_weight,
    neigh_bias,
    combine_weight,
    combine_bias,
    head_weight,
    head_bias,
    tail_weight,
    tail_bias,
    cotangent,
):
    row_count = lax.axis_size("rows")
    cols = lax.axis_size("cols")
    PLACE["me"] = jnp.stack([lax.axis_index("cols"), lax.axis_index("rows")]).astype(
        jnp.int32
    )
    pool_size = pull_rows.shape[1]
    capacity = pool_size // row_count
    nodes, channels = pin_feats.shape
    width = neigh_weight.shape[1]
    square = 2 * nodes * width * channels
    spread_flops = 2 * nodes * pool_size * channels
    block = (nodes, channels)
    lanes = (nodes // 128, 128)
    middle = row_count // 2
    half_outs = [((capacity, channels), bf16)] * (row_count // 2)
    block_outs = [(block, bf16)] * cols
    row_vector = ((1, channels), f32)

    def terms(sets, blocks, grad, scale=None):
        rows = sum(b.shape[1] for b in blocks)
        keep, send, sums = call(
            form(terms_kernel, sets, row_count),
            [((rows // 2, channels), bf16)] * 2 + [row_vector],
            *blocks,
            grad,
            *(() if scale is None else (scale,)),
            flops=2 * nodes * rows * channels,
        )
        return Going([(row_count // 2, rows // row_count)], keep, send, 0), sums

    def both_terms(blocks, grad, other_blocks, other_grad, scale):
        pieces, rows = [], 0
        for run in (blocks, other_blocks):
            count = sum(b.shape[1] for b in run)
            pieces.append((row_count // 2, count // row_count))
            rows += count // 2
        keep, send, sums, other_sums = call(
            form(both_kernel, len(blocks), len(other_blocks), row_count),
            [((rows, channels), bf16)] * 2 + [row_vector] * 2,
            *blocks,
            grad,
            *other_blocks,
            other_grad,
            scale,
            flops=4 * nodes * rows * channels,
        )
        return Going(pieces, keep, send, 0), sums, other_sums

    def both_halves(matrix, first):
        value, *sent = first
        rest = call(rest_kernel, half_outs, value, matrix, flops=spread_flops // 2)
        return sent + list(rest)

    requested = row_exchange(pull_rows.reshape(row_count, capacity)).reshape(-1)
    board_blocks = gather_cols(board_feats)
    kinds = (node_kinds == 1).astype(f32).reshape(lanes)
    proj_in, proj_bias_in, pins = copy_in(
        (proj_weight, None, None), (proj_bias[None], None, None), (pin_feats, None, None)
    )
    (hidden,) = call(
        form(board_kernel, cols, False),
        [(block, bf16)],
        *board_blocks,
        proj_in,
        proj_bias_in,
        pins,
        kinds,
        flops=square // 2,
    )
    hidden, requested = tie(hidden, requested)
    share = nodes // 2
    counted, visits = (
        lax.dynamic_slice_in_dim(a, lax.axis_index("cols") % 2 * share, share)
        for a in gate([neighbours, visit_counts], hidden)
    )
    dense = dense_counts(counted, visits, pool_size)
    (own_counts,) = call(flat_kernel, [((share, pool_size), bf16)], dense)
    local = jnp.arange(nodes, dtype=jnp.int32)
    selector = (requested[:, None] == local[None, :]).astype(bf16)
    (neigh_w0,) = copy_in((gate([neigh_weight], hidden)[0], 0, None))
    inv_total = (1.0 / jnp.sum(visit_counts.astype(f32), axis=1)).reshape(lanes)

    blocks_0, (neigh_w0, selector, own_counts) = gather_cols(
        hidden, (neigh_w0, selector, own_counts)
    )
    sent = both_halves(
        selector,
        call(
            form(neigh_kernel, cols, False),
            [(block, bf16)] + half_outs,
            *blocks_0,
            neigh_w0,
            neigh_bias[0:1],
            selector,
            flops=square + spread_flops // 2,
        ),
    )
    chunks = exchange(sent)
    (
        neigh_w1,
        self_w0,
        self_w1,
        gather_w0,
        gather_w1,
        head_w,
        tail_w,
        neigh_b,
        combine_b,
        head_b,
        tail_b,
        cotangent,
    ) = copy_in(
        (gate([neigh_weight], sent[-1])[0], 1, None),
        (combine_weight, 0, (0, width)),
        (combine_weight, 1, (0, width)),
        (combine_weight, 0, (width, 2 * width)),
        (combine_weight, 1, (width, 2 * width)),
        (head_weight, None, None),
        (tail_weight, None, None),
        (neigh_bias, None, None),
        (combine_bias, None, None),
        (head_bias[None], None, None),
        (tail_bias[None], None, None),
        (cotangent, None, None),
    )
    late = gate(blocks_0, sent[-1])
    counts, counts_t = call(
        counts_kernel,
        [((nodes, pool_size), bf16), ((pool_size, nodes), bf16)],
        own_counts,
        swap(*gate([own_counts], sent[-1]), "cols", 1),
    )
    self_raw_0, neigh_pre_0 = call(
        form(neigh_save_kernel, cols, False),
        [(block, f32), (block, f32)],
        *late,
        neigh_w0,
        neigh_b[0:1],
        self_w0,
        flops=2 * square,
    )
    *chunks, self_raw_0, neigh_pre_0 = tie(*chunks, self_raw_0, neigh_pre_0)
    (gathered,) = call(
        form(aggregate_kernel, row_count),
        [(block, bf16)],
        *chunks,
        counts,
        inv_total,
        flops=spread_flops,
    )
    (board_pre,) = call(
        form(board_kernel, cols, True),
        [(block, f32)],
        *gate(board_blocks, gathered),
        proj_in,
        proj_bias_in,
        flops=square // 2,
    )
    gathered_0, (board_pre,) = gather_cols(gathered, (board_pre,))
    fixed = (gather_w0, combine_b[0:1], self_raw_0)
    (act,) = call(
        form(combine_kernel, cols, False, False),
        [(block, bf16)],
        *gathered_0,
        *fixed,
        flops=square,
    )
    (combine_pre_0,) = call(
        form(combine_kernel, cols, False, True),
        [(block, f32)],
        *gate([*gathered_0, *fixed], act),
        flops=square,
    )

    blocks_1, (combine_pre_0,) = gather_cols(act, (combine_pre_0,))
    sent = both_halves(
        selector,
        call(
            form(neigh_kernel, cols, True),
            [(block, bf16)] + half_outs,
            *blocks_1,
            neigh_w1,
            neigh_b[1:2],
            selector,
            flops=square + spread_flops // 2,
        ),
    )
    chunks = exchange(sent)
    *late, requested_late = gate([*blocks_1, requested], sent[-1])
    inner_near, pairs = pair_sums(
        call(rt_kernel, block_outs, *gate([cotangent], sent[-1]), tail_w, flops=square)
    )
    inner_parts = parts_of(inner_near, pairs)
    self_raw_1, neigh_pre_1, scale_1, neigh_raw_1 = call(
        form(neigh_save_kernel, cols, True),
        [(block, f32), (block, f32), (lanes, f32), (block, f32)],
        *late,
        neigh_w1,
        neigh_b[1:2],
        self_w1,
        flops=2 * square,
    )
    select_t = (local[:, None] == requested_late[None, :]).astype(bf16)
    *chunks, self_raw_1, neigh_pre_1, scale_1, neigh_raw_1, select_t = tie(
        *chunks, self_raw_1, neigh_pre_1, scale_1, neigh_raw_1, select_t
    )
    (gathered,) = call(
        form(aggregate_kernel, row_count),
        [(block, bf16)],
        *chunks,
        counts,
        inv_total,
        flops=spread_flops,
    )
    gathered_1, inner_parts = gather_cols(gathered, inner_parts)
    fixed = (gather_w1, combine_b[1:2], self_raw_1, scale_1)
    (act,) = call(
        form(combine_kernel, cols, True, False),
        [(block, bf16)],
        *gathered_1,
        *fixed,
        flops=square,
    )
    (combine_pre_1,) = call(
        form(combine_kernel, cols, True, True),
        [(block, f32)],
        *gate([*gathered_1, *fixed], act),
        flops=square,
    )

    blocks_2, (combine_pre_1,) = gather_cols(act, (combine_pre_1,))
    *blocks, dot, head_grad, scale_2, inner_act = call(
        form(head_kernel, cols),
        block_outs + [(lanes, f32), (block, bf16), (lanes, f32), (block, bf16)],
        *blocks_2,
        *inner_parts,
        head_w,
        head_b,
        flops=3 * square,
    )
    near, pairs, dot = pair_sums(blocks, dot)
    head_going, head_bias_grad = terms(
        [(cols, True)], blocks_2, *gate([head_grad], pairs[0]), scale_2
    )
    parts, (head_going.keep,) = parts_of(near, pairs, (head_going.keep,))
    dots = all_chips(dot)

    def combine_back(parts, dots, weight, scale, pre):
        *blocks, grad = call(
            form(combine_back_kernel, cols, width),
            block_outs + [(block, bf16)],
            *parts,
            *dots,
            weight,
            scale,
            pre,
            flops=square,
        )
        return grad, *pair_sums(blocks)

    def pool_back(parts):
        return both_halves(
            counts_t,
            call(
                form(pool_back_kernel, cols),
                [(block, bf16)] + half_outs,
                *parts,
                counts_t,
                inv_total,
                flops=spread_flops // 2,
            ),
        )

    combine_grad, near, pairs = combine_back(
        parts, dots, gather_w1, scale_2, combine_pre_1
    )
    head_going = fold(head_going.after(pairs[0]))
    parts, (head_going.keep,) = parts_of(near, pairs, (head_going.keep,))
    sent = pool_back(parts)
    chunks = exchange(sent)
    (inner_late,) = gate([inner_act], sent[-1])
    (combine_late,) = gate([combine_grad], *chunks[: middle + 1])
    combine_going, combine_bias_1 = terms(
        [(cols, True), (cols, False)], [*blocks_1, *gathered_1], combine_late, scale_1
    )
    inner_blocks = gather_cols(inner_late, chunks[: middle + 1])[0]
    tail_rows = (width // 2, channels)
    tail_keep, tail_send, tail_bias_grad, embeddings = call(
        form(tail_kernel, cols, row_count),
        [(tail_rows, bf16), (tail_rows, bf16), row_vector],
        *inner_blocks,
        tail_w,
        tail_b,
        cotangent,
        saved=[(block, f32)],
        flops=2 * square,
    )
    *chunks, combine_going.keep = tie(*chunks, combine_going.keep)

    neigh_in = (select_t, neigh_pre_1, combine_grad, self_w1, neigh_w1)
    *blocks, neigh_grad_1, dot = call(
        form(neigh_back_kernel, row_count, cols, True),
        block_outs + [(block, bf16), (lanes, f32)],
        *chunks,
        *neigh_in,
        self_raw_1,
        neigh_raw_1,
        flops=spread_flops + 2 * square,
    )
    near, pairs, dot = pair_sums(blocks, dot)
    head_going = fold(head_going.after(pairs[0]))
    combine_going = fold(combine_going.after(pairs[0]))
    tail_keep, tail_send = gate([tail_keep, tail_send], pairs[0])
    tail_going = Going([(row_count // 2, width // row_count)], tail_keep, tail_send, 0)
    parts, (combine_going.keep, head_going.keep) = parts_of(
        near, pairs, (combine_going.keep, head_going.keep)
    )
    dots = all_chips(dot)

    combine_grad, near, pairs = combine_back(
        parts, dots, gather_w0, scale_1, combine_pre_0
    )
    first_going = fold(combine_going.after(pairs[0]))
    tail_going = fold(tail_going.after(pairs[0]))
    parts, (tail_going.keep, head_going.came, first_going.keep) = parts_of(
        near, pairs, (tail_going.keep, head_going.came, first_going.keep)
    )
    sent = pool_back(parts)
    chunks = exchange(sent)
    combine_late, neigh_late = gate([combine_grad, neigh_grad_1], sent[-1])
    combine_going, combine_bias_0, neigh_bias_1 = both_terms(
        [*blocks_0, *gathered_0], combine_late, blocks_1, neigh_late, scale_1
    )

    neigh_in = (select_t, neigh_pre_0, combine_grad, self_w0, neigh_w0)
    *blocks, neigh_grad = call(
        form(neigh_back_kernel, row_count, cols, False),
        block_outs + [(block, bf16)],
        *chunks,
        *neigh_in,
        flops=spread_flops + 2 * square,
    )
    near, pairs = pair_sums(blocks)
    second_going = fold(combine_going.after(pairs[0]))
    neigh_going_0, neigh_bias_0 = terms(
        [(cols, False)], blocks_0, *gate([neigh_grad], pairs[0])
    )
    parts, (second_going.keep, neigh_going_0.keep, first_going.came, tail_going.came) = (
        parts_of(
            near,
            pairs,
            (second_going.keep, neigh_going_0.keep, first_going.came, tail_going.came),
        )
    )

    board_block = ((nodes, board_feats.shape[1]), bf16)
    proj_rows = proj_weight.shape[0]
    pieces = [(row_count // 2, proj_rows // row_count), VECTORS]
    *blocks, keep, send, _, grad_pin = call(
        form(board_back_kernel, cols, row_count),
        [board_block] * cols + [((rows_of(pieces), channels), bf16)] * 2 + [row_vector],
        *parts,
        *board_blocks,
        board_pre,
        kinds,
        proj_in,
        neigh_bias_0,
        neigh_bias_1,
        combine_bias_0,
        combine_bias_1,
        head_bias_grad,
        tail_bias_grad,
        saved=[(block, f32)],
        flops=square,
    )
    proj_going = Going(pieces, keep, send, 0)
    third_going = fold(second_going.after(keep), tail_going.after(keep))
    last_going = fold(neigh_going_0.after(keep), proj_going)
    near, pairs = pair_sums(blocks)
    grad_board = sum(p.astype(f32) for p in parts_of(near, pairs))
    (head_out,), (combine_out_1,) = close(head_going), close(first_going)
    combine_out_0, neigh_out_1, tail_out = close(third_going)
    neigh_out_0, proj_out, biases = close(last_going)
    return (
        embeddings,
        grad_pin,
        grad_board,
        proj_out,
        biases[6],
        jnp.stack([neigh_out_0, neigh_out_1]),
        biases[0:2],
        jnp.stack([combine_out_0, combine_out_1]),
        biases[2:4],
        head_out,
        biases[4],
        tail_out,
        biases[5],
    )


def solution(mesh):
    placed = (
        P("rows", "cols"),
        P("rows", "cols"),
        P("rows"),
        P("rows", None),
        P("rows", None),
        P("rows", None),
        P(None, "cols"),
        P("cols"),
        P(None, None, "cols"),
        P(None, "cols"),
        P(None, None, "cols"),
        P(None, "cols"),
        P(None, "cols"),
        P("cols"),
        P(None, "cols"),
        P("cols"),
        P("rows", "cols"),
    )
    return jax.shard_map(
        body,
        mesh=mesh,
        in_specs=placed,
        out_specs=(
            P("rows", "cols"),
            P("rows", "cols"),
            P("rows", "cols"),
            P("rows", "cols"),
            P("cols"),
            P(None, "rows", "cols"),
            P(None, "cols"),
            P(None, "rows", "cols"),
            P(None, "cols"),
            P("rows", "cols"),
            P("cols"),
            P("rows", "cols"),
            P("cols"),
        ),
        check_vma=False,
    )
```

```python
import jax
import jax.numpy as jnp
from jax import lax
from jax.experimental import pallas as pl
from jax.experimental.pallas import tpu as pltpu
from jax.sharding import PartitionSpec as P

eps = 1e-06
bf16 = jnp.bfloat16
f32 = jnp.float32
MIB = 1 << 20
PLACE = {}


def tie(*arrays):
    return lax.optimization_barrier(arrays)


def gate(arrays, *tokens):
    return list(tie(*arrays, *tokens)[: len(arrays)])


def product(left_side, right_side):
    return jnp.dot(left_side, right_side, preferred_element_type=f32)


def product_t(left_side, right_side):
    return lax.dot_general(
        left_side, right_side, (((0,), (0,)), ((), ())), preferred_element_type=f32
    )


def product_rt(left_side, right_side):
    return lax.dot_general(
        left_side, right_side, (((1,), (1,)), ((), ())), preferred_element_type=f32
    )


def tanh_of(x):
    return jnp.tanh(0.7978845608028654 * (x + 0.044715 * (x * x * x)))


def gelu(x):
    return 0.5 * x * (1.0 + tanh_of(x))


def gelu_grad(x):
    t = tanh_of(x)
    slope = 0.7978845608028654 * (1.0 + 0.134145 * (x * x))
    return 0.5 * (1.0 + t) + 0.5 * x * (1.0 - t * t) * slope


def swap(array, axis, distance):
    size = lax.axis_size(axis)
    return lax.ppermute(array, axis, [(i, i ^ distance) for i in range(size)])


def gather_cols(shard, beside=()):
    size = lax.axis_size("cols")
    far = [swap(shard, "cols", step) for step in range(2, size, 2)]
    if beside:
        tied = tie(*far, *beside)
        far, beside = tied[: len(far)], tied[len(far) :]
    blocks = []
    for block in [shard, *far]:
        blocks += [block, swap(block, "cols", 1)]
    return (blocks, beside) if beside else blocks


def pair_sums(blocks, dot=None):
    evens, odds = blocks[2::2], blocks[3::2]
    came = [swap(odd, "cols", 1) for odd in odds]
    near = [blocks[0], swap(blocks[1], "cols", 1)]
    outs = [(block.shape, bf16) for block in evens]
    if dot is None:
        return near, list(call(pair_kernel, outs, *evens, *came))
    *pairs, dot = call(
        pair_dot_kernel, outs + [(dot.shape, f32)], *evens, *came, dot, swap(dot, "cols", 1)
    )
    return near, pairs, dot


def parts_of(near, pairs, beside=()):
    far = [swap(pair, "cols", 2 * i + 2) for i, pair in enumerate(pairs)]
    parts = tie(*near, *far, *beside)
    count = 2 + len(far)
    return (parts[:count], parts[count:]) if beside else parts


def all_chips(dot):
    return [dot] + [
        swap(dot, "cols", far) for far in range(2, lax.axis_size("cols"), 2)
    ]


def row_exchange(chunks):
    return lax.all_to_all(chunks, "rows", split_axis=0, concat_axis=0, tiled=True)


def row_order():
    return list(reversed(range(lax.axis_size("rows"))))


def exchange(chunks):
    return [
        swap(chunk, "rows", k) if k else chunk for k, chunk in zip(row_order(), chunks)
    ]


class Going:
    def __init__(self, pieces, keep, send, level):
        self.pieces, self.keep, self.level = pieces, keep, level
        self.came = swap(send, "rows", 1 << level)

    def after(self, token):
        self.keep, self.came = gate([self.keep, self.came], token)
        return self


VECTORS = (0, 16)


def halves(pieces):
    return [(n // 2, m) for n, m in pieces]


def rows_of(pieces):
    return sum(n * m if n else m for n, m in pieces)


def fold(*goings):
    pieces = [p for going in goings for p in going.pieces]
    level = goings[0].level + 1
    half = halves(pieces)
    shape = (rows_of(half), goings[0].keep.shape[1])
    arrays = [a for going in goings for a in (going.keep, going.came)]
    kernel = form(fold_kernel, [going.pieces for going in goings], level)
    keep, send = call(kernel, [(shape, bf16)] * 2, *arrays)
    return Going(half, keep, send, level)


def close(going):
    while going.pieces[0][0] > 1:
        going = fold(going)
    total = going.keep.astype(f32) + going.came.astype(f32)
    outs, at = [], 0
    for n, m in going.pieces:
        part = total[at : at + m]
        outs.append(part if n else part[: m // 2] + part[m // 2 :])
        at += m
    return outs


def form(kernel, *options):
    def run(*refs):
        kernel(*options, *refs)

    run.__name__ = kernel.__name__
    return run


def call(kernel, outs, *ins, saved=(), scratch=(), flops=0):
    vmem = pl.BlockSpec(memory_space=pltpu.VMEM)
    shapes = [jax.ShapeDtypeStruct(shape, dtype) for shape, dtype in outs]
    placed = [pltpu.HBM(shape, dtype) for shape, dtype in saved]
    size = sum(a.size * a.dtype.itemsize for a in ins)
    size += sum(jnp.dtype(t).itemsize * n[0] * n[1] for n, t in list(outs) + list(saved))
    extra = sum(jnp.dtype(t).itemsize * n[0] * n[1] for n, t in saved)

    def run(me_ref, *refs):
        if not saved:
            kernel(me_ref, *refs)
            return
        inner = len(ins) + len(outs)
        count = len(saved)
        targets, held = refs[inner : inner + count], refs[inner + count : -1]
        kernel(me_ref, *refs[:inner], *held)
        copies = [
            pltpu.make_async_copy(held[i], targets[i], refs[-1].at[i])
            for i in range(count)
        ]
        for copy in copies:
            copy.start()
        for copy in copies:
            copy.wait()

    return pl.pallas_call(
        run,
        out_shape=shapes + placed,
        in_specs=[pl.BlockSpec(memory_space=pltpu.SMEM)] + [vmem] * len(ins),
        out_specs=[vmem] * len(shapes)
        + [pl.BlockSpec(memory_space=pltpu.HBM)] * len(placed),
        scratch_shapes=[pltpu.VMEM(shape, dtype) for shape, dtype in [*saved, *scratch]]
        + ([pltpu.SemaphoreType.DMA((len(saved),))] if saved else []),
        cost_estimate=pl.CostEstimate(flops=flops, bytes_accessed=size, transcendentals=0),
        compiler_params=pltpu.CompilerParams(
            vmem_limit_bytes=max(12 * MIB, size * 5 // 4 + extra + 6 * MIB)
        ),
        name=kernel.__name__,
    )(PLACE["me"], *ins)


def copy_in(*parts):
    arrays = [part[0] for part in parts]
    count = len(parts)
    shapes = []
    for array, index, rows in parts:
        size = array.shape[-2] if rows is None else rows[1] - rows[0]
        shapes.append(jax.ShapeDtypeStruct((size, array.shape[-1]), array.dtype))

    def run(*refs):
        sems = refs[-1]
        copies = []
        for i, (array, index, rows) in enumerate(parts):
            source = refs[i] if index is None else refs[i].at[index]
            if rows is not None:
                source = source.at[pl.ds(rows[0], rows[1] - rows[0])]
            copies.append(pltpu.make_async_copy(source, refs[count + i], sems.at[i]))
        for copy in copies:
            copy.start()
        for copy in copies:
            copy.wait()

    size = sum(s.size * s.dtype.itemsize for s in shapes)
    return pl.pallas_call(
        run,
        out_shape=shapes,
        in_specs=[pl.BlockSpec(memory_space=pltpu.HBM)] * count,
        out_specs=[pl.BlockSpec(memory_space=pltpu.VMEM)] * count,
        scratch_shapes=[pltpu.SemaphoreType.DMA((count,))],
        cost_estimate=pl.CostEstimate(flops=0, bytes_accessed=size, transcendentals=0),
        compiler_params=pltpu.CompilerParams(vmem_limit_bytes=size * 2 + 4 * MIB),
    )(*[pltpu.with_memory_space_constraint(a, pltpu.HBM) for a in arrays])


def block_rows(me_ref, j, size):
    return pl.ds(pl.multiple_of((me_ref[0] ^ j) * size, size), size)


def sum_refs(refs):
    total = refs[0][...].astype(f32)
    for ref in refs[1:]:
        total = total + ref[...].astype(f32)
    return total


def blocks_product(me_ref, block_refs, weight_ref):
    total = None
    for j, ref in enumerate(block_refs):
        rows = block_rows(me_ref, j, ref.shape[1])
        term = product(ref[...], weight_ref[rows, :])
        total = term if total is None else total + term
    return total


def blocks_scale(block_refs):
    total = None
    for ref in block_refs:
        wide = ref[...].astype(f32)
        term = jnp.sum(wide * wide, axis=1, keepdims=True)
        total = term if total is None else total + term
    return lax.rsqrt(total / (len(block_refs) * block_refs[0].shape[1]) + eps)


def lane_mask():
    return lax.broadcasted_iota(jnp.int32, (128, 128), 0) == lax.broadcasted_iota(
        jnp.int32, (128, 128), 1
    )


def to_lanes(column, out_ref):
    mask = lane_mask()
    for i in range(out_ref.shape[0]):
        part = jnp.where(mask, column[i * 128 : (i + 1) * 128], 0.0)
        out_ref[i : i + 1, :] = jnp.sum(part, axis=0, keepdims=True)


def from_lanes(rows):
    mask = lane_mask()
    return jnp.concatenate(
        [
            jnp.sum(jnp.where(mask, rows[i : i + 1, :], 0.0), axis=1, keepdims=True)
            for i in range(rows.shape[0])
        ],
        axis=0,
    )


def pair_kernel(me_ref, *refs):
    count = len(refs) // 3
    for one, other, out in zip(refs[:count], refs[count : 2 * count], refs[2 * count :]):
        out[...] = (one[...].astype(f32) + other[...].astype(f32)).astype(bf16)


def pair_dot_kernel(me_ref, *refs):
    count = (len(refs) - 3) // 3
    blocks, rest = refs[: 2 * count], refs[2 * count :]
    pair_kernel(me_ref, *blocks, *rest[2 : 2 + count])
    rest[-1][...] = rest[0][...] + rest[1][...]


def flat_kernel(me_ref, dense, out):
    nodes = out.shape[0]
    groups = dense.shape[0] // nodes
    for h in range(groups):
        part = dense[pl.ds(h, nodes, stride=groups), :]
        out[:, h * 128 : (h + 1) * 128] = part.astype(bf16)


def counts_kernel(me_ref, own, other, out, out_t):
    core = me_ref[0] & 1
    size = own.shape[0]
    for ref, place in ((own, core), (other, 1 - core)):
        rows = pl.ds(pl.multiple_of(place * size, size), size)
        value = ref[...]
        out[rows, :] = value
        out_t[:, rows] = value.T


def board_kernel(count, save, me_ref, *refs):
    blocks, refs = refs[:count], refs[count:]
    weight, bias, *refs = refs
    pre = blocks_product(me_ref, blocks, weight) + bias[...]
    if save:
        refs[0][...] = pre
        return
    pin, kinds, hidden_out = refs
    board = from_lanes(kinds) > 0.5
    hidden_out[...] = jnp.where(board, gelu(pre), pin[...].astype(f32)).astype(bf16)


def chunk_span(me_ref, k, size):
    return pl.ds(pl.multiple_of((me_ref[1] ^ k) * size, size), size)


def send_chunks(me_ref, matrix, value, outs, first):
    for i, out in enumerate(outs):
        rows = chunk_span(me_ref, first - i, out.shape[0])
        out[...] = product(matrix[rows, :], value).astype(bf16)


def rest_kernel(me_ref, value, matrix, *outs):
    send_chunks(me_ref, matrix, value[...], outs, len(outs) - 1)


def take_chunks(me_ref, matrix, chunks):
    total = None
    for k, ref in zip(reversed(range(len(chunks))), chunks):
        term = product(matrix[:, chunk_span(me_ref, k, ref.shape[0])], ref[...])
        total = term if total is None else total + term
    return total


def neigh_kernel(count, scaled, me_ref, *refs):
    blocks, refs = refs[:count], refs[count:]
    weight, bias, selector, moved_out, *outs = refs
    pre = blocks_product(me_ref, blocks, weight)
    if scaled:
        pre = blocks_scale(blocks) * pre
    moved = gelu(pre + bias[...]).astype(bf16)
    moved_out[...] = moved
    send_chunks(me_ref, selector, moved, outs, 2 * len(outs) - 1)


def neigh_save_kernel(count, scaled, me_ref, *refs):
    blocks, refs = refs[:count], refs[count:]
    weight, bias, self_w, self_out, pre_out, *refs = refs
    raw = blocks_product(me_ref, blocks, weight)
    if scaled:
        scale_out, raw_out = refs
        scale = blocks_scale(blocks)
        to_lanes(scale, scale_out)
        raw_out[...] = raw
        pre_out[...] = scale * raw + bias[...]
    else:
        pre_out[...] = raw + bias[...]
    self_out[...] = blocks_product(me_ref, blocks, self_w)


def aggregate_kernel(count, me_ref, *refs):
    chunks, (counts, inv_total, out) = refs[:count], refs[count:]
    total = take_chunks(me_ref, counts, chunks)
    out[...] = (total * from_lanes(inv_total)).astype(bf16)


def combine_kernel(count, scaled, save, me_ref, *refs):
    blocks, refs = refs[:count], refs[count:]
    weight, bias, self_raw, *refs = refs
    pre = blocks_product(me_ref, blocks, weight)
    own = self_raw[...]
    if scaled:
        own = from_lanes(refs[0]) * own
    pre = own + pre + bias[...]
    if save:
        refs[-1][...] = pre
    else:
        refs[-1][...] = gelu(pre).astype(bf16)


def blocks_rt(me_ref, pairs, outs):
    for j in reversed(range(len(outs))):
        rows = block_rows(me_ref, j, outs[j].shape[1])
        total = None
        for g, w in pairs:
            term = product_rt(g, w[rows, :])
            total = term if total is None else total + term
        outs[j][...] = total.astype(bf16)


def rt_kernel(me_ref, grad, weight, *outs):
    blocks_rt(me_ref, [(grad[...], weight)], outs)


def head_kernel(count, me_ref, *refs):
    blocks, refs = refs[:count], refs[count:]
    parts, refs = refs[: count // 2 + 1], refs[count // 2 + 1 :]
    weight, bias, *outs = refs
    outs, (dot_out, grad_out, scale_out, inner_out) = outs[:count], outs[count:]
    raw = blocks_product(me_ref, blocks, weight)
    scale = blocks_scale(blocks)
    to_lanes(scale, scale_out)
    pre = scale * raw + bias[...]
    inner_out[...] = gelu(pre).astype(bf16)
    grad = (sum_refs(parts) * gelu_grad(pre)).astype(bf16)
    grad_out[...] = grad
    blocks_rt(me_ref, [(grad, weight)], outs)
    to_lanes(jnp.sum(raw * grad.astype(f32), axis=1, keepdims=True), dot_out)


def combine_back_kernel(count, width, me_ref, *refs):
    parts, refs = refs[: count // 2 + 1], refs[count // 2 + 1 :]
    dots, refs = refs[: count // 2], refs[count // 2 :]
    weight, scale, pre, *outs, grad_out = refs
    dot = sum_refs(dots)
    scale, pre = from_lanes(scale), pre[...]
    factor = scale * scale * scale * from_lanes(dot) / width
    act_grad = scale * sum_refs(parts) - gelu(pre) * factor
    grad = (act_grad * gelu_grad(pre)).astype(bf16)
    grad_out[...] = grad
    blocks_rt(me_ref, [(grad, weight)], outs)


def pool_back_kernel(count, me_ref, *refs):
    parts, refs = refs[: count // 2 + 1], refs[count // 2 + 1 :]
    counts_t, inv_total, grad_out, *outs = refs
    grad = (sum_refs(parts) * from_lanes(inv_total)).astype(bf16)
    grad_out[...] = grad
    send_chunks(me_ref, counts_t, grad, outs, 2 * len(outs) - 1)


def neigh_back_kernel(count, cols, dotted, me_ref, *refs):
    chunks, refs = refs[:count], refs[count:]
    select_t, pre, combine_grad, self_w, weight, *refs = refs
    grad = (take_chunks(me_ref, select_t, chunks) * gelu_grad(pre[...])).astype(bf16)
    own = combine_grad[...]
    if dotted:
        self_raw, raw, *refs = refs
        dot = self_raw[...] * own.astype(f32) + raw[...] * grad.astype(f32)
        to_lanes(jnp.sum(dot, axis=1, keepdims=True), refs[-1])
    refs[cols][...] = grad
    blocks_rt(me_ref, [(own, self_w), (grad, weight)], refs[:cols])


def board_back_kernel(count, row_count, me_ref, *refs):
    parts, refs = refs[: count // 2 + 1], refs[count // 2 + 1 :]
    blocks, refs = refs[:count], refs[count:]
    pre, kinds, *biases = refs
    biases, (keep, send, sums, grad_out) = biases[:6], biases[6:]
    board = from_lanes(kinds) > 0.5
    wide = jnp.where(board, sum_refs(parts), 0.0) * gelu_grad(pre[...])
    grad = wide.astype(bf16)
    grad_out[...] = grad
    rows = keep.shape[0] - 16
    terms_kernel(
        [(count, False)],
        row_count,
        False,
        me_ref,
        *blocks,
        grad,
        keep.at[pl.ds(0, rows)],
        send.at[pl.ds(0, rows)],
        sums,
    )
    last = sums[...]
    stacked = [ref[...] for ref in biases] + [last, jnp.zeros_like(last)]
    stacked = split_vectors(jnp.concatenate(stacked, axis=0))
    keep[rows : rows + 16, :] = stacked
    send[rows : rows + 16, :] = stacked


def board_rest_kernel(count, me_ref, *refs):
    parts, (kinds, grad, weight, *refs) = refs[: count // 2 + 1], refs[count // 2 + 1 :]
    outs, (pin_out,) = refs[:count], refs[count:]
    blocks_rt(me_ref, [(grad[...], weight)], outs)
    pin_out[...] = jnp.where(from_lanes(kinds) > 0.5, 0.0, sum_refs(parts))


def place_piece(stay, keep, send, at, value):
    rows = pl.ds(pl.multiple_of(at, 16), value.shape[0])

    @pl.when(stay)
    def _():
        keep[rows, :] = value

    @pl.when(jnp.logical_not(stay))
    def _():
        send[rows, :] = value


def terms_kernel(sets, row_count, joined, me_ref, *refs):
    *refs, keep, send, sum_out = refs
    count = sum(n for n, _ in sets)
    blocks, refs = refs[:count], refs[count:]
    if joined:
        rows = sum(ref.shape[1] for ref in blocks) // 2
        for other, out in zip(refs[-2:], (keep, send)):
            out[pl.ds(rows, other.shape[0]), :] = other[...]
    grad = refs[0][...]
    wide = grad.astype(f32)
    sum_out[...] = jnp.sum(wide, axis=0, keepdims=True)
    total = sum(ref.shape[1] for ref in blocks)
    chunk = total // row_count
    bit = me_ref[1] & 1
    base = 0
    for n, scaled in sets:
        value = (from_lanes(refs[1]) * wide).astype(bf16) if scaled else grad
        for j in range(n):
            ref = blocks[j]
            size = ref.shape[1]
            part = product_t(ref[...], value).astype(bf16)
            step = min(size, chunk)
            first = base + (me_ref[0] ^ j) * size
            for i in range(size // step):
                start = first + i * step
                q = start // chunk
                at = (q // 2) * chunk + start % chunk
                stay = (q & 1) == bit
                place_piece(stay, keep, send, at, part[i * step : (i + 1) * step])
        base += sum(ref.shape[1] for ref in blocks[:n])
        blocks = blocks[n:]


def tail_kernel(count, row_count, me_ref, *refs):
    blocks, refs = refs[:count], refs[count:]
    weight, bias, cotangent, keep, send, sum_out, out = refs
    out[...] = blocks_product(me_ref, blocks, weight) + bias[...]
    terms_kernel(
        [(count, False)],
        row_count,
        False,
        me_ref,
        *blocks,
        cotangent,
        keep,
        send,
        sum_out,
    )


def split_vectors(values):
    high = values.astype(bf16).astype(f32)
    return jnp.concatenate([high, values - high], axis=0).astype(bf16)


def fold_kernel(groups, level, me_ref, *refs):
    *refs, keep, send = refs
    bit = (me_ref[1] >> level) & 1
    base = 0
    for i, pieces in enumerate(groups):
        one, other = refs[2 * i], refs[2 * i + 1]
        at = 0
        for n, m in pieces:
            if n == 0:
                span = slice(at, at + m)
                total = one[span, :].astype(f32) + other[span, :].astype(f32)
                total = split_vectors(total[: m // 2] + total[m // 2 :])
                keep[base : base + m, :] = total
                send[base : base + m, :] = total
                at += m
                base += m
            for q in range(0, n, 2):
                rows = slice(base + (q // 2) * m, base + (q // 2 + 1) * m)
                for out, place in ((keep, bit), (send, 1 - bit)):
                    span = pl.ds(pl.multiple_of(at + (q + place) * m, 16), m)
                    total = one[span, :].astype(f32) + other[span, :].astype(f32)
                    out[rows, :] = total.astype(bf16)
            at += n * m
            base += (n // 2) * m


def dense_counts(neighbours, visit_counts, pool_size):
    low_width = 128
    high_width = pool_size // low_width
    upper_idx = neighbours // low_width
    lower_idx = neighbours % low_width
    upper_hot = jnp.where(
        upper_idx[:, :, None] == jnp.arange(high_width, dtype=jnp.int32)[None, None, :],
        visit_counts[:, :, None],
        0,
    ).astype(bf16)
    lower_hot = (
        lower_idx[:, :, None] == jnp.arange(low_width, dtype=jnp.int32)[None, None, :]
    ).astype(bf16)
    dense = jnp.einsum("vkh,vkl->vhl", upper_hot, lower_hot, preferred_element_type=f32)
    return dense.reshape(-1, low_width)


def body(
    pin_feats,
    board_feats,
    node_kinds,
    neighbours,
    visit_counts,
    pull_rows,
    proj_weight,
    proj_bias,
    neigh_weight,
    neigh_bias,
    combine_weight,
    combine_bias,
    head_weight,
    head_bias,
    tail_weight,
    tail_bias,
    cotangent,
):
    row_count = lax.axis_size("rows")
    cols = lax.axis_size("cols")
    PLACE["me"] = jnp.stack([lax.axis_index("cols"), lax.axis_index("rows")]).astype(
        jnp.int32
    )
    pool_size = pull_rows.shape[1]
    capacity = pool_size // row_count
    nodes, channels = pin_feats.shape
    width = neigh_weight.shape[1]
    square = 2 * nodes * width * channels
    spread_flops = 2 * nodes * pool_size * channels
    block = (nodes, channels)
    lanes = (nodes // 128, 128)
    middle = row_count // 2
    half_outs = [((capacity, channels), bf16)] * (row_count // 2)
    block_outs = [(block, bf16)] * cols
    row_vector = ((1, channels), f32)

    def term_halves(sets, blocks, grad, scale=None, joined=None):
        rows = sum(b.shape[1] for b in blocks)
        pieces, others = ([], ()) if joined is None else joined
        pieces = [(row_count // 2, rows // row_count), *pieces]
        keep, send, sums = call(
            form(terms_kernel, sets, row_count, joined is not None),
            [((rows_of(pieces), channels), bf16)] * 2 + [row_vector],
            *blocks,
            grad,
            *(() if scale is None else (scale,)),
            *others,
            flops=2 * nodes * rows * channels,
        )
        return pieces, [keep, send], sums

    def terms(*args, joined=None):
        pieces, halves_of, sums = term_halves(*args, joined=joined)
        return Going(pieces, *halves_of, 0), sums

    def both_halves(matrix, first):
        value, *sent = first
        rest = call(rest_kernel, half_outs, value, matrix, flops=spread_flops // 2)
        return sent + list(rest)

    requested = row_exchange(pull_rows.reshape(row_count, capacity)).reshape(-1)
    board_blocks = gather_cols(board_feats)
    kinds = (node_kinds == 1).astype(f32).reshape(lanes)
    proj_in, proj_bias_in, pins = copy_in(
        (proj_weight, None, None), (proj_bias[None], None, None), (pin_feats, None, None)
    )
    (hidden,) = call(
        form(board_kernel, cols, False),
        [(block, bf16)],
        *board_blocks,
        proj_in,
        proj_bias_in,
        pins,
        kinds,
        flops=square // 2,
    )
    hidden, requested = tie(hidden, requested)
    share = nodes // 2
    counted, visits = (
        lax.dynamic_slice_in_dim(a, lax.axis_index("cols") % 2 * share, share)
        for a in gate([neighbours, visit_counts], hidden)
    )
    dense = dense_counts(counted, visits, pool_size)
    local = jnp.arange(nodes, dtype=jnp.int32)
    selector = (requested[:, None] == local[None, :]).astype(bf16)
    (neigh_w0,) = copy_in((gate([neigh_weight], hidden)[0], 0, None))
    inv_total = (1.0 / jnp.sum(visit_counts.astype(f32), axis=1)).reshape(lanes)

    blocks_0, (neigh_w0, selector, dense) = gather_cols(
        hidden, (neigh_w0, selector, dense)
    )
    (own_counts,) = call(
        flat_kernel, [((share, pool_size), bf16)], *gate([dense], blocks_0[2])
    )
    *blocks_0, own_counts = tie(*blocks_0, own_counts)
    other_counts = swap(own_counts, "cols", 1)
    sent = both_halves(
        selector,
        call(
            form(neigh_kernel, cols, False),
            [(block, bf16)] + half_outs,
            *blocks_0,
            neigh_w0,
            neigh_bias[0:1],
            selector,
            flops=square + spread_flops // 2,
        ),
    )
    chunks = exchange(sent)
    counts, counts_t = call(
        counts_kernel,
        [((nodes, pool_size), bf16), ((pool_size, nodes), bf16)],
        own_counts,
        other_counts,
    )
    (gathered,) = call(
        form(aggregate_kernel, row_count),
        [(block, bf16)],
        *chunks,
        counts,
        inv_total,
        flops=spread_flops,
    )
    self_w0, gather_w0, neigh_b, combine_b = copy_in(
        (gate([combine_weight], gathered)[0], 0, (0, width)),
        (combine_weight, 0, (width, 2 * width)),
        (neigh_bias, None, None),
        (combine_bias, None, None),
    )
    self_raw_0, neigh_pre_0 = call(
        form(neigh_save_kernel, cols, False),
        [(block, f32), (block, f32)],
        *gate(blocks_0, gathered),
        neigh_w0,
        neigh_b[0:1],
        self_w0,
        flops=2 * square,
    )
    gathered_0, (self_raw_0, neigh_pre_0, gather_w0) = gather_cols(
        gathered, (self_raw_0, neigh_pre_0, gather_w0)
    )
    fixed = (gather_w0, combine_b[0:1], self_raw_0)
    (act,) = call(
        form(combine_kernel, cols, False, False),
        [(block, bf16)],
        *gathered_0,
        *fixed,
        flops=square,
    )
    (combine_pre_0,) = call(
        form(combine_kernel, cols, False, True),
        [(block, f32)],
        *gate([*gathered_0, *fixed], act),
        flops=square,
    )
    (neigh_w1, *weights) = copy_in(
        (gate([neigh_weight], act)[0], 1, None),
        (combine_weight, 1, (0, width)),
        (combine_weight, 1, (width, 2 * width)),
        (head_weight, None, None),
        (tail_weight, None, None),
        (head_bias[None], None, None),
        (tail_bias[None], None, None),
        (cotangent, None, None),
    )

    blocks_1, (combine_pre_0, neigh_w1, *weights) = gather_cols(
        act, (combine_pre_0, neigh_w1, *weights)
    )
    self_w1, gather_w1, head_w, tail_w, head_b, tail_b, cotangent = weights
    sent = both_halves(
        selector,
        call(
            form(neigh_kernel, cols, True),
            [(block, bf16)] + half_outs,
            *blocks_1,
            neigh_w1,
            neigh_b[1:2],
            selector,
            flops=square + spread_flops // 2,
        ),
    )
    chunks = exchange(sent)
    inner_near, pairs = pair_sums(
        call(rt_kernel, block_outs, *gate([cotangent], sent[-1]), tail_w, flops=square)
    )
    inner_parts = parts_of(inner_near, pairs)
    (gathered,) = call(
        form(aggregate_kernel, row_count),
        [(block, bf16)],
        *chunks,
        counts,
        inv_total,
        flops=spread_flops,
    )
    *late, requested_late = gate([*blocks_1, requested], gathered)
    self_raw_1, neigh_pre_1, scale_1, neigh_raw_1 = call(
        form(neigh_save_kernel, cols, True),
        [(block, f32), (block, f32), (lanes, f32), (block, f32)],
        *late,
        neigh_w1,
        neigh_b[1:2],
        self_w1,
        flops=2 * square,
    )
    select_t = (local[:, None] == requested_late[None, :]).astype(bf16)
    (board_pre,) = call(
        form(board_kernel, cols, True),
        [(block, f32)],
        *gate(board_blocks, gathered),
        proj_in,
        proj_bias_in,
        flops=square // 2,
    )
    gathered_1, (self_raw_1, neigh_pre_1, scale_1, neigh_raw_1, select_t, board_pre) = (
        gather_cols(
            gathered,
            (self_raw_1, neigh_pre_1, scale_1, neigh_raw_1, select_t, board_pre),
        )
    )
    fixed = (gather_w1, combine_b[1:2], self_raw_1, scale_1)
    (act,) = call(
        form(combine_kernel, cols, True, False),
        [(block, bf16)],
        *gathered_1,
        *fixed,
        flops=square,
    )
    (combine_pre_1,) = call(
        form(combine_kernel, cols, True, True),
        [(block, f32)],
        *gate([*gathered_1, *fixed], act),
        flops=square,
    )

    blocks_2, (combine_pre_1, *inner_parts) = gather_cols(
        act, (combine_pre_1, *inner_parts)
    )
    *blocks, dot, head_grad, scale_2, inner_act = call(
        form(head_kernel, cols),
        block_outs + [(lanes, f32), (block, bf16), (lanes, f32), (block, bf16)],
        *blocks_2,
        *inner_parts,
        head_w,
        head_b,
        flops=3 * square,
    )
    near, pairs, dot = pair_sums(blocks, dot)
    head_going, head_bias_grad = terms(
        [(cols, True)], blocks_2, *gate([head_grad], pairs[0]), scale_2
    )
    parts, (head_going.keep,) = parts_of(near, pairs, (head_going.keep,))
    dots = all_chips(dot)

    def combine_back(parts, dots, weight, scale, pre):
        *blocks, grad = call(
            form(combine_back_kernel, cols, width),
            block_outs + [(block, bf16)],
            *parts,
            *dots,
            weight,
            scale,
            pre,
            flops=square,
        )
        return grad, *pair_sums(blocks)

    def pool_back(parts):
        return both_halves(
            counts_t,
            call(
                form(pool_back_kernel, cols),
                [(block, bf16)] + half_outs,
                *parts,
                counts_t,
                inv_total,
                flops=spread_flops // 2,
            ),
        )

    combine_grad, near, pairs = combine_back(
        parts, dots, gather_w1, scale_2, combine_pre_1
    )
    combine_going, combine_bias_1 = terms(
        [(cols, True), (cols, False)],
        [*blocks_1, *gathered_1],
        *gate([combine_grad], pairs[0]),
        scale_1,
    )
    parts, (combine_going.keep,) = parts_of(near, pairs, (combine_going.keep,))
    sent = pool_back(parts)
    chunks = exchange(sent)
    inner_blocks = gather_cols(*gate([inner_act], sent[-1]))
    *chunks, inner_blocks[-2] = tie(*chunks, inner_blocks[-2])

    neigh_in = (select_t, neigh_pre_1, combine_grad, self_w1, neigh_w1)
    *blocks, neigh_grad_1, dot = call(
        form(neigh_back_kernel, row_count, cols, True),
        block_outs + [(block, bf16), (lanes, f32)],
        *chunks,
        *neigh_in,
        self_raw_1,
        neigh_raw_1,
        flops=spread_flops + 2 * square,
    )
    near, pairs, dot = pair_sums(blocks, dot)
    first_going = fold(head_going.after(pairs[0]), combine_going.after(pairs[0]))
    tail_rows = (width // 2, channels)
    tail_keep, tail_send, tail_bias_grad, embeddings = call(
        form(tail_kernel, cols, row_count),
        [(tail_rows, bf16), (tail_rows, bf16), row_vector],
        *gate(inner_blocks, pairs[0]),
        tail_w,
        tail_b,
        cotangent,
        saved=[(block, f32)],
        flops=2 * square,
    )
    parts, (first_going.keep, tail_keep) = parts_of(
        near, pairs, (first_going.keep, tail_keep)
    )
    dots = all_chips(dot)

    combine_grad, near, pairs = combine_back(
        parts, dots, gather_w0, scale_1, combine_pre_0
    )
    combine_going, combine_bias_0 = terms(
        [(cols, False), (cols, False)],
        [*blocks_0, *gathered_0],
        *gate([combine_grad], pairs[0]),
        joined=([(row_count // 2, width // row_count)], (tail_keep, tail_send)),
    )
    parts, (combine_going.keep,) = parts_of(near, pairs, (combine_going.keep,))
    sent = pool_back(parts)
    chunks = exchange(sent)
    pieces_1, halves_1, neigh_bias_1 = term_halves(
        [(cols, True)], blocks_1, *gate([neigh_grad_1], sent[-1]), scale_1
    )
    *chunks, halves_1[0] = tie(*chunks, halves_1[0])

    neigh_in = (select_t, neigh_pre_0, combine_grad, self_w0, neigh_w0)
    *blocks, neigh_grad = call(
        form(neigh_back_kernel, row_count, cols, False),
        block_outs + [(block, bf16)],
        *chunks,
        *neigh_in,
        flops=spread_flops + 2 * square,
    )
    near, pairs = pair_sums(blocks)
    first_going = fold(first_going.after(pairs[0]))
    second_going = fold(combine_going.after(pairs[0]))
    neigh_going_0, neigh_bias_0 = terms(
        [(cols, False)],
        blocks_0,
        *gate([neigh_grad], pairs[0]),
        joined=(pieces_1, halves_1),
    )
    parts, (second_going.keep, neigh_going_0.keep, first_going.keep) = parts_of(
        near, pairs, (second_going.keep, neigh_going_0.keep, first_going.keep)
    )

    board_block = ((nodes, board_feats.shape[1]), bf16)
    proj_rows = proj_weight.shape[0]
    pieces = [(row_count // 2, proj_rows // row_count), VECTORS]
    keep, send, _, board_grad = call(
        form(board_back_kernel, cols, row_count),
        [((rows_of(pieces), channels), bf16)] * 2 + [row_vector, (block, bf16)],
        *parts,
        *board_blocks,
        board_pre,
        kinds,
        neigh_bias_0,
        neigh_bias_1,
        combine_bias_0,
        combine_bias_1,
        head_bias_grad,
        tail_bias_grad,
        flops=square // 2,
    )
    third_going = fold(second_going.after(keep))
    proj_going = Going(pieces, keep, send, 0)
    last_going = fold(neigh_going_0.after(keep), proj_going)
    *blocks, grad_pin = call(
        form(board_rest_kernel, cols),
        [board_block] * cols,
        *gate(parts, last_going.keep),
        kinds,
        board_grad,
        proj_in,
        saved=[(block, f32)],
        flops=square // 2,
    )
    near, pairs = pair_sums(blocks)
    grad_board = sum(p.astype(f32) for p in parts_of(near, pairs))
    head_out, combine_out_1 = close(first_going)
    combine_out_0, tail_out = close(third_going)
    neigh_out_0, neigh_out_1, proj_out, biases = close(last_going)
    return (
        embeddings,
        grad_pin,
        grad_board,
        proj_out,
        biases[6],
        jnp.stack([neigh_out_0, neigh_out_1]),
        biases[0:2],
        jnp.stack([combine_out_0, combine_out_1]),
        biases[2:4],
        head_out,
        biases[4],
        tail_out,
        biases[5],
    )


def solution(mesh):
    placed = (
        P("rows", "cols"),
        P("rows", "cols"),
        P("rows"),
        P("rows", None),
        P("rows", None),
        P("rows", None),
        P(None, "cols"),
        P("cols"),
        P(None, None, "cols"),
        P(None, "cols"),
        P(None, None, "cols"),
        P(None, "cols"),
        P(None, "cols"),
        P("cols"),
        P(None, "cols"),
        P("cols"),
        P("rows", "cols"),
    )
    return jax.shard_map(
        body,
        mesh=mesh,
        in_specs=placed,
        out_specs=(
            P("rows", "cols"),
            P("rows", "cols"),
            P("rows", "cols"),
            P("rows", "cols"),
            P("cols"),
            P(None, "rows", "cols"),
            P(None, "cols"),
            P(None, "rows", "cols"),
            P(None, "cols"),
            P("rows", "cols"),
            P("cols"),
            P("rows", "cols"),
            P("cols"),
        ),
        check_vma=False,
    )
```

```python
import jax
import jax.numpy as jnp
from jax import lax
from jax.experimental import pallas as pl
from jax.experimental.pallas import tpu as pltpu
from jax.sharding import PartitionSpec as P

eps = 1e-06
bf16 = jnp.bfloat16
f32 = jnp.float32
MIB = 1 << 20
PLACE = {}


def tie(*arrays):
    return lax.optimization_barrier(arrays)


def gate(arrays, *tokens):
    return list(tie(*arrays, *tokens)[: len(arrays)])


def product(left_side, right_side):
    return jnp.dot(left_side, right_side, preferred_element_type=f32)


def product_t(left_side, right_side):
    return lax.dot_general(
        left_side, right_side, (((0,), (0,)), ((), ())), preferred_element_type=f32
    )


def product_rt(left_side, right_side):
    return lax.dot_general(
        left_side, right_side, (((1,), (1,)), ((), ())), preferred_element_type=f32
    )


def tanh_of(x):
    return jnp.tanh(0.7978845608028654 * (x + 0.044715 * (x * x * x)))


def gelu(x):
    return 0.5 * x * (1.0 + tanh_of(x))


def gelu_grad(x):
    t = tanh_of(x)
    slope = 0.7978845608028654 * (1.0 + 0.134145 * (x * x))
    return 0.5 * (1.0 + t) + 0.5 * x * (1.0 - t * t) * slope


def swap(array, axis, distance):
    size = lax.axis_size(axis)
    return lax.ppermute(array, axis, [(i, i ^ distance) for i in range(size)])


def gather_cols(shard, beside=()):
    size = lax.axis_size("cols")
    far = [swap(shard, "cols", step) for step in range(2, size, 2)]
    if beside:
        tied = tie(*far, *beside)
        far, beside = tied[: len(far)], tied[len(far) :]
    blocks = []
    for block in [shard, *far]:
        blocks += [block, swap(block, "cols", 1)]
    return (blocks, beside) if beside else blocks


def pair_sums(blocks, dot=None):
    evens, odds = blocks[2::2], blocks[3::2]
    came = [swap(odd, "cols", 1) for odd in odds]
    near = [blocks[0], swap(blocks[1], "cols", 1)]
    outs = [(block.shape, bf16) for block in evens]
    if dot is None:
        return near, list(call(pair_kernel, outs, *evens, *came))
    *pairs, dot = call(
        pair_dot_kernel, outs + [(dot.shape, f32)], *evens, *came, dot, swap(dot, "cols", 1)
    )
    return near, pairs, dot


def parts_of(near, pairs, beside=()):
    far = [swap(pair, "cols", 2 * i + 2) for i, pair in enumerate(pairs)]
    parts = tie(*near, *far, *beside)
    count = 2 + len(far)
    return (parts[:count], parts[count:]) if beside else parts


def all_chips(dot):
    return [dot] + [
        swap(dot, "cols", far) for far in range(2, lax.axis_size("cols"), 2)
    ]


def row_exchange(chunks):
    return lax.all_to_all(chunks, "rows", split_axis=0, concat_axis=0, tiled=True)


def row_order():
    return list(reversed(range(lax.axis_size("rows"))))


def exchange(chunks):
    return [
        swap(chunk, "rows", k) if k else chunk for k, chunk in zip(row_order(), chunks)
    ]


class Going:
    def __init__(self, pieces, keep, send, level):
        self.pieces, self.keep, self.level = pieces, keep, level
        self.came = swap(send, "rows", 1 << level)

    def after(self, token):
        self.keep, self.came = gate([self.keep, self.came], token)
        return self


VECTORS = (0, 16)


def halves(pieces):
    return [(n // 2, m) for n, m in pieces]


def rows_of(pieces):
    return sum(n * m if n else m for n, m in pieces)


def fold(*goings):
    pieces = [p for going in goings for p in going.pieces]
    level = goings[0].level + 1
    half = halves(pieces)
    shape = (rows_of(half), goings[0].keep.shape[1])
    arrays = [a for going in goings for a in (going.keep, going.came)]
    kernel = form(fold_kernel, [going.pieces for going in goings], level)
    keep, send = call(kernel, [(shape, bf16)] * 2, *arrays)
    return Going(half, keep, send, level)


def close(going):
    while going.pieces[0][0] > 1:
        going = fold(going)
    total = going.keep.astype(f32) + going.came.astype(f32)
    outs, at = [], 0
    for n, m in going.pieces:
        part = total[at : at + m]
        outs.append(part if n else part[: m // 2] + part[m // 2 :])
        at += m
    return outs


def form(kernel, *options):
    def run(*refs):
        kernel(*options, *refs)

    run.__name__ = kernel.__name__
    return run


def call(kernel, outs, *ins, saved=(), scratch=(), flops=0):
    vmem = pl.BlockSpec(memory_space=pltpu.VMEM)
    shapes = [jax.ShapeDtypeStruct(shape, dtype) for shape, dtype in outs]
    placed = [pltpu.HBM(shape, dtype) for shape, dtype in saved]
    size = sum(a.size * a.dtype.itemsize for a in ins)
    size += sum(jnp.dtype(t).itemsize * n[0] * n[1] for n, t in list(outs) + list(saved))
    extra = sum(jnp.dtype(t).itemsize * n[0] * n[1] for n, t in saved)

    def run(me_ref, *refs):
        if not saved:
            kernel(me_ref, *refs)
            return
        inner = len(ins) + len(outs)
        count = len(saved)
        targets, held = refs[inner : inner + count], refs[inner + count : -1]
        kernel(me_ref, *refs[:inner], *held)
        copies = [
            pltpu.make_async_copy(held[i], targets[i], refs[-1].at[i])
            for i in range(count)
        ]
        for copy in copies:
            copy.start()
        for copy in copies:
            copy.wait()

    return pl.pallas_call(
        run,
        out_shape=shapes + placed,
        in_specs=[pl.BlockSpec(memory_space=pltpu.SMEM)] + [vmem] * len(ins),
        out_specs=[vmem] * len(shapes)
        + [pl.BlockSpec(memory_space=pltpu.HBM)] * len(placed),
        scratch_shapes=[pltpu.VMEM(shape, dtype) for shape, dtype in [*saved, *scratch]]
        + ([pltpu.SemaphoreType.DMA((len(saved),))] if saved else []),
        cost_estimate=pl.CostEstimate(flops=flops, bytes_accessed=size, transcendentals=0),
        compiler_params=pltpu.CompilerParams(
            vmem_limit_bytes=max(12 * MIB, size * 5 // 4 + extra + 6 * MIB)
        ),
        name=kernel.__name__,
    )(PLACE["me"], *ins)


def copy_in(*parts):
    arrays = [part[0] for part in parts]
    count = len(parts)
    shapes = []
    for array, index, rows in parts:
        size = array.shape[-2] if rows is None else rows[1] - rows[0]
        shapes.append(jax.ShapeDtypeStruct((size, array.shape[-1]), array.dtype))

    def run(*refs):
        sems = refs[-1]
        copies = []
        for i, (array, index, rows) in enumerate(parts):
            source = refs[i] if index is None else refs[i].at[index]
            if rows is not None:
                source = source.at[pl.ds(rows[0], rows[1] - rows[0])]
            copies.append(pltpu.make_async_copy(source, refs[count + i], sems.at[i]))
        for copy in copies:
            copy.start()
        for copy in copies:
            copy.wait()

    size = sum(s.size * s.dtype.itemsize for s in shapes)
    return pl.pallas_call(
        run,
        out_shape=shapes,
        in_specs=[pl.BlockSpec(memory_space=pltpu.HBM)] * count,
        out_specs=[pl.BlockSpec(memory_space=pltpu.VMEM)] * count,
        scratch_shapes=[pltpu.SemaphoreType.DMA((count,))],
        cost_estimate=pl.CostEstimate(flops=0, bytes_accessed=size, transcendentals=0),
        compiler_params=pltpu.CompilerParams(vmem_limit_bytes=size * 2 + 4 * MIB),
    )(*[pltpu.with_memory_space_constraint(a, pltpu.HBM) for a in arrays])


def block_rows(me_ref, j, size):
    return pl.ds(pl.multiple_of((me_ref[0] ^ j) * size, size), size)


def sum_refs(refs):
    total = refs[0][...].astype(f32)
    for ref in refs[1:]:
        total = total + ref[...].astype(f32)
    return total


def blocks_product(me_ref, block_refs, weight_ref):
    total = None
    for j, ref in enumerate(block_refs):
        rows = block_rows(me_ref, j, ref.shape[1])
        term = product(ref[...], weight_ref[rows, :])
        total = term if total is None else total + term
    return total


def blocks_scale(block_refs):
    total = None
    for ref in block_refs:
        wide = ref[...].astype(f32)
        term = jnp.sum(wide * wide, axis=1, keepdims=True)
        total = term if total is None else total + term
    return lax.rsqrt(total / (len(block_refs) * block_refs[0].shape[1]) + eps)


def lane_mask():
    return lax.broadcasted_iota(jnp.int32, (128, 128), 0) == lax.broadcasted_iota(
        jnp.int32, (128, 128), 1
    )


def to_lanes(column, out_ref):
    mask = lane_mask()
    for i in range(out_ref.shape[0]):
        part = jnp.where(mask, column[i * 128 : (i + 1) * 128], 0.0)
        out_ref[i : i + 1, :] = jnp.sum(part, axis=0, keepdims=True)


def from_lanes(rows):
    mask = lane_mask()
    return jnp.concatenate(
        [
            jnp.sum(jnp.where(mask, rows[i : i + 1, :], 0.0), axis=1, keepdims=True)
            for i in range(rows.shape[0])
        ],
        axis=0,
    )


def pair_kernel(me_ref, *refs):
    count = len(refs) // 3
    for one, other, out in zip(refs[:count], refs[count : 2 * count], refs[2 * count :]):
        out[...] = (one[...].astype(f32) + other[...].astype(f32)).astype(bf16)


def pair_dot_kernel(me_ref, *refs):
    count = (len(refs) - 3) // 3
    blocks, rest = refs[: 2 * count], refs[2 * count :]
    pair_kernel(me_ref, *blocks, *rest[2 : 2 + count])
    rest[-1][...] = rest[0][...] + rest[1][...]


def flat_kernel(me_ref, dense, out):
    nodes = out.shape[0]
    groups = dense.shape[0] // nodes
    for h in range(groups):
        part = dense[pl.ds(h, nodes, stride=groups), :]
        out[:, h * 128 : (h + 1) * 128] = part.astype(bf16)


def counts_kernel(me_ref, own, other, out, out_t):
    core = me_ref[0] & 1
    size = own.shape[0]
    for ref, place in ((own, core), (other, 1 - core)):
        rows = pl.ds(pl.multiple_of(place * size, size), size)
        value = ref[...]
        out[rows, :] = value
        out_t[:, rows] = value.T


def board_kernel(count, save, me_ref, *refs):
    blocks, refs = refs[:count], refs[count:]
    weight, bias, *refs = refs
    pre = blocks_product(me_ref, blocks, weight) + bias[...]
    if save:
        refs[0][...] = pre
        return
    pin, kinds, hidden_out = refs
    board = from_lanes(kinds) > 0.5
    hidden_out[...] = jnp.where(board, gelu(pre), pin[...].astype(f32)).astype(bf16)


def chunk_span(me_ref, k, size):
    return pl.ds(pl.multiple_of((me_ref[1] ^ k) * size, size), size)


def send_chunks(me_ref, matrix, value, outs, first):
    for i, out in enumerate(outs):
        rows = chunk_span(me_ref, first - i, out.shape[0])
        out[...] = product(matrix[rows, :], value).astype(bf16)


def rest_kernel(me_ref, value, matrix, *outs):
    send_chunks(me_ref, matrix, value[...], outs, len(outs) - 1)


def take_chunks(me_ref, matrix, chunks):
    total = None
    for k, ref in zip(reversed(range(len(chunks))), chunks):
        term = product(matrix[:, chunk_span(me_ref, k, ref.shape[0])], ref[...])
        total = term if total is None else total + term
    return total


def neigh_kernel(count, scaled, me_ref, *refs):
    blocks, refs = refs[:count], refs[count:]
    weight, bias, selector, moved_out, *outs = refs
    pre = blocks_product(me_ref, blocks, weight)
    if scaled:
        pre = blocks_scale(blocks) * pre
    moved = gelu(pre + bias[...]).astype(bf16)
    moved_out[...] = moved
    send_chunks(me_ref, selector, moved, outs, 2 * len(outs) - 1)


def neigh_save_kernel(count, scaled, me_ref, *refs):
    blocks, refs = refs[:count], refs[count:]
    weight, bias, self_w, self_out, pre_out, *refs = refs
    raw = blocks_product(me_ref, blocks, weight)
    if scaled:
        scale_out, raw_out = refs
        scale = blocks_scale(blocks)
        to_lanes(scale, scale_out)
        raw_out[...] = raw
        pre_out[...] = scale * raw + bias[...]
    else:
        pre_out[...] = raw + bias[...]
    self_out[...] = blocks_product(me_ref, blocks, self_w)


def aggregate_kernel(count, me_ref, *refs):
    chunks, (counts, inv_total, out) = refs[:count], refs[count:]
    total = take_chunks(me_ref, counts, chunks)
    out[...] = (total * from_lanes(inv_total)).astype(bf16)


def combine_kernel(count, scaled, save, me_ref, *refs):
    blocks, refs = refs[:count], refs[count:]
    weight, bias, self_raw, *refs = refs
    pre = blocks_product(me_ref, blocks, weight)
    own = self_raw[...]
    if scaled:
        own = from_lanes(refs[0]) * own
    pre = own + pre + bias[...]
    if save:
        refs[-1][...] = pre
    else:
        refs[-1][...] = gelu(pre).astype(bf16)


def blocks_rt(me_ref, pairs, outs):
    for j in reversed(range(len(outs))):
        rows = block_rows(me_ref, j, outs[j].shape[1])
        total = None
        for g, w in pairs:
            term = product_rt(g, w[rows, :])
            total = term if total is None else total + term
        outs[j][...] = total.astype(bf16)


def rt_kernel(me_ref, grad, weight, *outs):
    blocks_rt(me_ref, [(grad[...], weight)], outs)


def head_kernel(count, me_ref, *refs):
    blocks, refs = refs[:count], refs[count:]
    parts, refs = refs[: count // 2 + 1], refs[count // 2 + 1 :]
    weight, bias, *outs = refs
    outs, (dot_out, grad_out, scale_out, inner_out) = outs[:count], outs[count:]
    raw = blocks_product(me_ref, blocks, weight)
    scale = blocks_scale(blocks)
    to_lanes(scale, scale_out)
    pre = scale * raw + bias[...]
    inner_out[...] = gelu(pre).astype(bf16)
    grad = (sum_refs(parts) * gelu_grad(pre)).astype(bf16)
    grad_out[...] = grad
    blocks_rt(me_ref, [(grad, weight)], outs)
    to_lanes(jnp.sum(raw * grad.astype(f32), axis=1, keepdims=True), dot_out)


def combine_back_kernel(count, width, me_ref, *refs):
    parts, refs = refs[: count // 2 + 1], refs[count // 2 + 1 :]
    dots, refs = refs[: count // 2], refs[count // 2 :]
    weight, scale, pre, *outs, grad_out = refs
    dot = sum_refs(dots)
    scale, pre = from_lanes(scale), pre[...]
    factor = scale * scale * scale * from_lanes(dot) / width
    act_grad = scale * sum_refs(parts) - gelu(pre) * factor
    grad = (act_grad * gelu_grad(pre)).astype(bf16)
    grad_out[...] = grad
    blocks_rt(me_ref, [(grad, weight)], outs)


def pool_back_kernel(count, me_ref, *refs):
    parts, refs = refs[: count // 2 + 1], refs[count // 2 + 1 :]
    counts_t, inv_total, grad_out, *outs = refs
    grad = (sum_refs(parts) * from_lanes(inv_total)).astype(bf16)
    grad_out[...] = grad
    send_chunks(me_ref, counts_t, grad, outs, 2 * len(outs) - 1)


def neigh_back_kernel(count, cols, dotted, me_ref, *refs):
    chunks, refs = refs[:count], refs[count:]
    select_t, pre, combine_grad, self_w, weight, *refs = refs
    grad = (take_chunks(me_ref, select_t, chunks) * gelu_grad(pre[...])).astype(bf16)
    own = combine_grad[...]
    if dotted:
        self_raw, raw, *refs = refs
        dot = self_raw[...] * own.astype(f32) + raw[...] * grad.astype(f32)
        to_lanes(jnp.sum(dot, axis=1, keepdims=True), refs[-1])
    refs[cols][...] = grad
    blocks_rt(me_ref, [(own, self_w), (grad, weight)], refs[:cols])


def board_back_kernel(count, row_count, me_ref, *refs):
    parts, refs = refs[: count // 2 + 1], refs[count // 2 + 1 :]
    blocks, refs = refs[:count], refs[count:]
    pre, kinds, *biases = refs
    biases, (keep, send, sums, grad_out) = biases[:6], biases[6:]
    board = from_lanes(kinds) > 0.5
    wide = jnp.where(board, sum_refs(parts), 0.0) * gelu_grad(pre[...])
    grad = wide.astype(bf16)
    grad_out[...] = grad
    rows = keep.shape[0] - 16
    terms_kernel(
        [(count, False)],
        row_count,
        False,
        me_ref,
        *blocks,
        grad,
        keep.at[pl.ds(0, rows)],
        send.at[pl.ds(0, rows)],
        sums,
    )
    last = sums[...]
    stacked = [ref[...] for ref in biases] + [last, jnp.zeros_like(last)]
    stacked = split_vectors(jnp.concatenate(stacked, axis=0))
    keep[rows : rows + 16, :] = stacked
    send[rows : rows + 16, :] = stacked


def board_rest_kernel(count, me_ref, *refs):
    parts, (kinds, grad, weight, *refs) = refs[: count // 2 + 1], refs[count // 2 + 1 :]
    outs, (pin_out,) = refs[:count], refs[count:]
    blocks_rt(me_ref, [(grad[...], weight)], outs)
    pin_out[...] = jnp.where(from_lanes(kinds) > 0.5, 0.0, sum_refs(parts))


def place_piece(stay, keep, send, at, value):
    rows = pl.ds(pl.multiple_of(at, 16), value.shape[0])

    @pl.when(stay)
    def _():
        keep[rows, :] = value

    @pl.when(jnp.logical_not(stay))
    def _():
        send[rows, :] = value


def terms_kernel(sets, row_count, joined, me_ref, *refs):
    *refs, keep, send, sum_out = refs
    count = sum(n for n, _ in sets)
    blocks, refs = refs[:count], refs[count:]
    if joined:
        rows = sum(ref.shape[1] for ref in blocks) // 2
        for other, out in zip(refs[-2:], (keep, send)):
            out[pl.ds(rows, other.shape[0]), :] = other[...]
    grad = refs[0][...]
    wide = grad.astype(f32)
    sum_out[...] = jnp.sum(wide, axis=0, keepdims=True)
    total = sum(ref.shape[1] for ref in blocks)
    chunk = total // row_count
    bit = me_ref[1] & 1
    base = 0
    for n, scaled in sets:
        value = (from_lanes(refs[1]) * wide).astype(bf16) if scaled else grad
        for j in range(n):
            ref = blocks[j]
            size = ref.shape[1]
            part = product_t(ref[...], value).astype(bf16)
            step = min(size, chunk)
            first = base + (me_ref[0] ^ j) * size
            for i in range(size // step):
                start = first + i * step
                q = start // chunk
                at = (q // 2) * chunk + start % chunk
                stay = (q & 1) == bit
                place_piece(stay, keep, send, at, part[i * step : (i + 1) * step])
        base += sum(ref.shape[1] for ref in blocks[:n])
        blocks = blocks[n:]


def turn_kernel(count, me_ref, *refs):
    for blocks, out in zip(
        [refs[i : i + count] for i in range(0, len(refs) - len(refs) // (count + 1), count)],
        refs[-(len(refs) // (count + 1)) :],
    ):
        for j, ref in enumerate(blocks):
            out[block_rows(me_ref, j, ref.shape[1]), :] = ref[...].T


def turned_kernel(scaled, row_count, joined, me_ref, *refs):
    *refs, keep, send, sum_out = refs
    arrays, refs = refs[: len(scaled)], refs[len(scaled) :]
    rows = sum(ref.shape[0] for ref in arrays) // 2
    if joined:
        for other, out in zip(refs[-2:], (keep, send)):
            out[pl.ds(rows, other.shape[0]), :] = other[...]
    grad = refs[0][...]
    wide = grad.astype(f32)
    sum_out[...] = jnp.sum(wide, axis=0, keepdims=True)
    chunk = 2 * rows // row_count
    bit = me_ref[1] & 1
    base = 0
    for ref, by_scale in zip(arrays, scaled):
        value = (from_lanes(refs[1]) * wide).astype(bf16) if by_scale else grad
        step = 2 * chunk
        for p in range(ref.shape[0] // step):
            at = base + p * chunk
            for out, place in ((keep, bit), (send, 1 - bit)):
                span = pl.ds(pl.multiple_of(p * step + place * chunk, 16), chunk)
                out[at : at + chunk, :] = product(ref[span, :], value).astype(bf16)
        base += ref.shape[0] // 2


def tail_kernel(count, row_count, me_ref, *refs):
    blocks, refs = refs[:count], refs[count:]
    weight, bias, cotangent, keep, send, sum_out, out = refs
    out[...] = blocks_product(me_ref, blocks, weight) + bias[...]
    terms_kernel(
        [(count, False)],
        row_count,
        False,
        me_ref,
        *blocks,
        cotangent,
        keep,
        send,
        sum_out,
    )


def split_vectors(values):
    high = values.astype(bf16).astype(f32)
    return jnp.concatenate([high, values - high], axis=0).astype(bf16)


def fold_kernel(groups, level, me_ref, *refs):
    *refs, keep, send = refs
    bit = (me_ref[1] >> level) & 1
    base = 0
    for i, pieces in enumerate(groups):
        one, other = refs[2 * i], refs[2 * i + 1]
        at = 0
        for n, m in pieces:
            if n == 0:
                span = slice(at, at + m)
                total = one[span, :].astype(f32) + other[span, :].astype(f32)
                total = split_vectors(total[: m // 2] + total[m // 2 :])
                keep[base : base + m, :] = total
                send[base : base + m, :] = total
                at += m
                base += m
            for q in range(0, n, 2):
                rows = slice(base + (q // 2) * m, base + (q // 2 + 1) * m)
                for out, place in ((keep, bit), (send, 1 - bit)):
                    span = pl.ds(pl.multiple_of(at + (q + place) * m, 16), m)
                    total = one[span, :].astype(f32) + other[span, :].astype(f32)
                    out[rows, :] = total.astype(bf16)
            at += n * m
            base += (n // 2) * m


def dense_counts(neighbours, visit_counts, pool_size):
    low_width = 128
    high_width = pool_size // low_width
    upper_idx = neighbours // low_width
    lower_idx = neighbours % low_width
    upper_hot = jnp.where(
        upper_idx[:, :, None] == jnp.arange(high_width, dtype=jnp.int32)[None, None, :],
        visit_counts[:, :, None],
        0,
    ).astype(bf16)
    lower_hot = (
        lower_idx[:, :, None] == jnp.arange(low_width, dtype=jnp.int32)[None, None, :]
    ).astype(bf16)
    dense = jnp.einsum("vkh,vkl->vhl", upper_hot, lower_hot, preferred_element_type=f32)
    return dense.reshape(-1, low_width)


def body(
    pin_feats,
    board_feats,
    node_kinds,
    neighbours,
    visit_counts,
    pull_rows,
    proj_weight,
    proj_bias,
    neigh_weight,
    neigh_bias,
    combine_weight,
    combine_bias,
    head_weight,
    head_bias,
    tail_weight,
    tail_bias,
    cotangent,
):
    row_count = lax.axis_size("rows")
    cols = lax.axis_size("cols")
    PLACE["me"] = jnp.stack([lax.axis_index("cols"), lax.axis_index("rows")]).astype(
        jnp.int32
    )
    pool_size = pull_rows.shape[1]
    capacity = pool_size // row_count
    nodes, channels = pin_feats.shape
    width = neigh_weight.shape[1]
    square = 2 * nodes * width * channels
    spread_flops = 2 * nodes * pool_size * channels
    block = (nodes, channels)
    lanes = (nodes // 128, 128)
    middle = row_count // 2
    half_outs = [((capacity, channels), bf16)] * (row_count // 2)
    block_outs = [(block, bf16)] * cols
    row_vector = ((1, channels), f32)

    def term_halves(sets, blocks, grad, scale=None, joined=None):
        rows = sum(b.shape[1] for b in blocks)
        pieces, others = ([], ()) if joined is None else joined
        pieces = [(row_count // 2, rows // row_count), *pieces]
        keep, send, sums = call(
            form(terms_kernel, sets, row_count, joined is not None),
            [((rows_of(pieces), channels), bf16)] * 2 + [row_vector],
            *blocks,
            grad,
            *(() if scale is None else (scale,)),
            *others,
            flops=2 * nodes * rows * channels,
        )
        return pieces, [keep, send], sums

    def terms(*args, joined=None):
        pieces, halves_of, sums = term_halves(*args, joined=joined)
        return Going(pieces, *halves_of, 0), sums

    def turn(*runs):
        return call(
            form(turn_kernel, cols),
            [((sum(b.shape[1] for b in run), nodes), bf16) for run in runs],
            *[b for run in runs for b in run],
        )

    def turned_halves(scaled, arrays, grad, scale=None, joined=None):
        rows = sum(a.shape[0] for a in arrays)
        pieces, others = ([], ()) if joined is None else joined
        pieces = [(row_count // 2, rows // row_count), *pieces]
        keep, send, sums = call(
            form(turned_kernel, scaled, row_count, joined is not None),
            [((rows_of(pieces), channels), bf16)] * 2 + [row_vector],
            *arrays,
            grad,
            *(() if scale is None else (scale,)),
            *others,
            flops=2 * nodes * rows * channels,
        )
        return pieces, [keep, send], sums

    def turned_terms(*args, joined=None):
        pieces, halves_of, sums = turned_halves(*args, joined=joined)
        return Going(pieces, *halves_of, 0), sums

    def both_halves(matrix, first):
        value, *sent = first
        rest = call(rest_kernel, half_outs, value, matrix, flops=spread_flops // 2)
        return sent + list(rest)

    requested = row_exchange(pull_rows.reshape(row_count, capacity)).reshape(-1)
    board_blocks = gather_cols(board_feats)
    kinds = (node_kinds == 1).astype(f32).reshape(lanes)
    proj_in, proj_bias_in, pins = copy_in(
        (proj_weight, None, None), (proj_bias[None], None, None), (pin_feats, None, None)
    )
    (hidden,) = call(
        form(board_kernel, cols, False),
        [(block, bf16)],
        *board_blocks,
        proj_in,
        proj_bias_in,
        pins,
        kinds,
        flops=square // 2,
    )
    hidden, requested = tie(hidden, requested)
    share = nodes // 2
    counted, visits = (
        lax.dynamic_slice_in_dim(a, lax.axis_index("cols") % 2 * share, share)
        for a in gate([neighbours, visit_counts], hidden)
    )
    dense = dense_counts(counted, visits, pool_size)
    local = jnp.arange(nodes, dtype=jnp.int32)
    selector = (requested[:, None] == local[None, :]).astype(bf16)
    (neigh_w0,) = copy_in((gate([neigh_weight], hidden)[0], 0, None))
    inv_total = (1.0 / jnp.sum(visit_counts.astype(f32), axis=1)).reshape(lanes)

    blocks_0, (neigh_w0, selector, dense) = gather_cols(
        hidden, (neigh_w0, selector, dense)
    )
    (own_counts,) = call(
        flat_kernel, [((share, pool_size), bf16)], *gate([dense], blocks_0[2])
    )
    *blocks_0, own_counts = tie(*blocks_0, own_counts)
    other_counts = swap(own_counts, "cols", 1)
    sent = both_halves(
        selector,
        call(
            form(neigh_kernel, cols, False),
            [(block, bf16)] + half_outs,
            *blocks_0,
            neigh_w0,
            neigh_bias[0:1],
            selector,
            flops=square + spread_flops // 2,
        ),
    )
    chunks = exchange(sent)
    counts, counts_t = call(
        counts_kernel,
        [((nodes, pool_size), bf16), ((pool_size, nodes), bf16)],
        own_counts,
        other_counts,
    )
    (turned_0,) = turn(gate(blocks_0, sent[-1]))
    *chunks, turned_0 = tie(*chunks, turned_0)
    (gathered,) = call(
        form(aggregate_kernel, row_count),
        [(block, bf16)],
        *chunks,
        counts,
        inv_total,
        flops=spread_flops,
    )
    self_w0, gather_w0, neigh_b, combine_b = copy_in(
        (gate([combine_weight], gathered)[0], 0, (0, width)),
        (combine_weight, 0, (width, 2 * width)),
        (neigh_bias, None, None),
        (combine_bias, None, None),
    )
    self_raw_0, neigh_pre_0 = call(
        form(neigh_save_kernel, cols, False),
        [(block, f32), (block, f32)],
        *gate(blocks_0, gathered),
        neigh_w0,
        neigh_b[0:1],
        self_w0,
        flops=2 * square,
    )
    gathered_0, (self_raw_0, neigh_pre_0, gather_w0) = gather_cols(
        gathered, (self_raw_0, neigh_pre_0, gather_w0)
    )
    fixed = (gather_w0, combine_b[0:1], self_raw_0)
    (act,) = call(
        form(combine_kernel, cols, False, False),
        [(block, bf16)],
        *gathered_0,
        *fixed,
        flops=square,
    )
    (combine_pre_0,) = call(
        form(combine_kernel, cols, False, True),
        [(block, f32)],
        *gate([*gathered_0, *fixed], act),
        flops=square,
    )
    (neigh_w1, *weights) = copy_in(
        (gate([neigh_weight], act)[0], 1, None),
        (combine_weight, 1, (0, width)),
        (combine_weight, 1, (width, 2 * width)),
        (head_weight, None, None),
        (tail_weight, None, None),
        (head_bias[None], None, None),
        (tail_bias[None], None, None),
        (cotangent, None, None),
    )

    blocks_1, (combine_pre_0, neigh_w1, *weights) = gather_cols(
        act, (combine_pre_0, neigh_w1, *weights)
    )
    self_w1, gather_w1, head_w, tail_w, head_b, tail_b, cotangent = weights
    sent = both_halves(
        selector,
        call(
            form(neigh_kernel, cols, True),
            [(block, bf16)] + half_outs,
            *blocks_1,
            neigh_w1,
            neigh_b[1:2],
            selector,
            flops=square + spread_flops // 2,
        ),
    )
    chunks = exchange(sent)
    inner_near, pairs = pair_sums(
        call(rt_kernel, block_outs, *gate([cotangent], sent[-1]), tail_w, flops=square)
    )
    inner_parts = parts_of(inner_near, pairs)
    turned_1, turned_gathered_0 = turn(
        gate(blocks_1, sent[-1]), gate(gathered_0, sent[-1])
    )
    *chunks, turned_1, turned_gathered_0 = tie(*chunks, turned_1, turned_gathered_0)
    (gathered,) = call(
        form(aggregate_kernel, row_count),
        [(block, bf16)],
        *chunks,
        counts,
        inv_total,
        flops=spread_flops,
    )
    *late, requested_late = gate([*blocks_1, requested], gathered)
    self_raw_1, neigh_pre_1, scale_1, neigh_raw_1 = call(
        form(neigh_save_kernel, cols, True),
        [(block, f32), (block, f32), (lanes, f32), (block, f32)],
        *late,
        neigh_w1,
        neigh_b[1:2],
        self_w1,
        flops=2 * square,
    )
    select_t = (local[:, None] == requested_late[None, :]).astype(bf16)
    (board_pre,) = call(
        form(board_kernel, cols, True),
        [(block, f32)],
        *gate(board_blocks, gathered),
        proj_in,
        proj_bias_in,
        flops=square // 2,
    )
    gathered_1, (self_raw_1, neigh_pre_1, scale_1, neigh_raw_1, select_t, board_pre) = (
        gather_cols(
            gathered,
            (self_raw_1, neigh_pre_1, scale_1, neigh_raw_1, select_t, board_pre),
        )
    )
    fixed = (gather_w1, combine_b[1:2], self_raw_1, scale_1)
    (act,) = call(
        form(combine_kernel, cols, True, False),
        [(block, bf16)],
        *gathered_1,
        *fixed,
        flops=square,
    )
    (combine_pre_1,) = call(
        form(combine_kernel, cols, True, True),
        [(block, f32)],
        *gate([*gathered_1, *fixed], act),
        flops=square,
    )

    (turned_gathered_1,) = turn(gate(gathered_1, act))
    blocks_2, (combine_pre_1, turned_gathered_1, *inner_parts) = gather_cols(
        act, (combine_pre_1, turned_gathered_1, *inner_parts)
    )
    *blocks, dot, head_grad, scale_2, inner_act = call(
        form(head_kernel, cols),
        block_outs + [(lanes, f32), (block, bf16), (lanes, f32), (block, bf16)],
        *blocks_2,
        *inner_parts,
        head_w,
        head_b,
        flops=3 * square,
    )
    near, pairs, dot = pair_sums(blocks, dot)
    head_going, head_bias_grad = terms(
        [(cols, True)], blocks_2, *gate([head_grad], pairs[0]), scale_2
    )
    parts, (head_going.keep,) = parts_of(near, pairs, (head_going.keep,))
    dots = all_chips(dot)

    def combine_back(parts, dots, weight, scale, pre):
        *blocks, grad = call(
            form(combine_back_kernel, cols, width),
            block_outs + [(block, bf16)],
            *parts,
            *dots,
            weight,
            scale,
            pre,
            flops=square,
        )
        return grad, *pair_sums(blocks)

    def pool_back(parts):
        return both_halves(
            counts_t,
            call(
                form(pool_back_kernel, cols),
                [(block, bf16)] + half_outs,
                *parts,
                counts_t,
                inv_total,
                flops=spread_flops // 2,
            ),
        )

    combine_grad, near, pairs = combine_back(
        parts, dots, gather_w1, scale_2, combine_pre_1
    )
    combine_going, combine_bias_1 = turned_terms(
        (True, False),
        [turned_1, turned_gathered_1],
        *gate([combine_grad], pairs[0]),
        scale_1,
    )
    parts, (combine_going.keep, head_going.came) = parts_of(
        near, pairs, (combine_going.keep, head_going.came)
    )
    sent = pool_back(parts)
    chunks = exchange(sent)
    inner_blocks = gather_cols(*gate([inner_act], sent[-1]))
    *chunks, inner_blocks[-2], combine_going.came = tie(
        *chunks, inner_blocks[-2], combine_going.came
    )

    neigh_in = (select_t, neigh_pre_1, combine_grad, self_w1, neigh_w1)
    *blocks, neigh_grad_1, dot = call(
        form(neigh_back_kernel, row_count, cols, True),
        block_outs + [(block, bf16), (lanes, f32)],
        *chunks,
        *neigh_in,
        self_raw_1,
        neigh_raw_1,
        flops=spread_flops + 2 * square,
    )
    near, pairs, dot = pair_sums(blocks, dot)
    first_going = fold(head_going.after(pairs[0]), combine_going.after(pairs[0]))
    tail_rows = (width // 2, channels)
    tail_keep, tail_send, tail_bias_grad, embeddings = call(
        form(tail_kernel, cols, row_count),
        [(tail_rows, bf16), (tail_rows, bf16), row_vector],
        *gate(inner_blocks, pairs[0]),
        tail_w,
        tail_b,
        cotangent,
        saved=[(block, f32)],
        flops=2 * square,
    )
    pieces_1, halves_1, neigh_bias_1 = turned_halves(
        (True,),
        [turned_1],
        *gate([neigh_grad_1], pairs[0]),
        scale_1,
        joined=([(row_count // 2, width // row_count)], (tail_keep, tail_send)),
    )
    parts, (first_going.keep, halves_1[0]) = parts_of(
        near, pairs, (first_going.keep, halves_1[0])
    )
    dots = all_chips(dot)

    combine_grad, near, pairs = combine_back(
        parts, dots, gather_w0, scale_1, combine_pre_0
    )
    combine_going, combine_bias_0 = turned_terms(
        (False, False),
        [turned_0, turned_gathered_0],
        combine_grad,
        joined=(pieces_1, halves_1),
    )
    parts, (combine_going.keep, first_going.came) = parts_of(
        near, pairs, (combine_going.keep, first_going.came)
    )
    sent = pool_back(parts)
    chunks = exchange(sent)

    neigh_in = (select_t, neigh_pre_0, combine_grad, self_w0, neigh_w0)
    *blocks, neigh_grad = call(
        form(neigh_back_kernel, row_count, cols, False),
        block_outs + [(block, bf16)],
        *chunks,
        *neigh_in,
        flops=spread_flops + 2 * square,
    )
    near, pairs = pair_sums(blocks)
    first_going = fold(first_going.after(pairs[0]))
    second_going = fold(combine_going.after(pairs[0]))
    neigh_going_0, neigh_bias_0 = turned_terms(
        (False,), [turned_0], *gate([neigh_grad], pairs[0])
    )
    parts, (second_going.keep, neigh_going_0.keep, first_going.keep) = parts_of(
        near, pairs, (second_going.keep, neigh_going_0.keep, first_going.keep)
    )

    board_block = ((nodes, board_feats.shape[1]), bf16)
    proj_rows = proj_weight.shape[0]
    pieces = [(row_count // 2, proj_rows // row_count), VECTORS]
    keep, send, _, board_grad = call(
        form(board_back_kernel, cols, row_count),
        [((rows_of(pieces), channels), bf16)] * 2 + [row_vector, (block, bf16)],
        *parts,
        *board_blocks,
        board_pre,
        kinds,
        neigh_bias_0,
        neigh_bias_1,
        combine_bias_0,
        combine_bias_1,
        head_bias_grad,
        tail_bias_grad,
        flops=square // 2,
    )
    proj_going = Going(pieces, keep, send, 0)
    last_going = fold(neigh_going_0.after(keep), proj_going)
    last_going.came, second_going.came = tie(last_going.came, second_going.came)
    third_going = fold(second_going)
    *blocks, grad_pin = call(
        form(board_rest_kernel, cols),
        [board_block] * cols,
        *gate(parts, last_going.came, third_going.keep),
        kinds,
        board_grad,
        proj_in,
        saved=[(block, f32)],
        flops=square // 2,
    )
    near, pairs = pair_sums(blocks)
    grad_board = sum(p.astype(f32) for p in parts_of(near, pairs))
    third_going.came, grad_board = tie(third_going.came, grad_board)
    head_out, combine_out_1 = close(first_going)
    combine_out_0, neigh_out_1, tail_out = close(third_going)
    neigh_out_0, proj_out, biases = close(last_going)
    return (
        embeddings,
        grad_pin,
        grad_board,
        proj_out,
        biases[6],
        jnp.stack([neigh_out_0, neigh_out_1]),
        biases[0:2],
        jnp.stack([combine_out_0, combine_out_1]),
        biases[2:4],
        head_out,
        biases[4],
        tail_out,
        biases[5],
    )


def solution(mesh):
    placed = (
        P("rows", "cols"),
        P("rows", "cols"),
        P("rows"),
        P("rows", None),
        P("rows", None),
        P("rows", None),
        P(None, "cols"),
        P("cols"),
        P(None, None, "cols"),
        P(None, "cols"),
        P(None, None, "cols"),
        P(None, "cols"),
        P(None, "cols"),
        P("cols"),
        P(None, "cols"),
        P("cols"),
        P("rows", "cols"),
    )
    return jax.shard_map(
        body,
        mesh=mesh,
        in_specs=placed,
        out_specs=(
            P("rows", "cols"),
            P("rows", "cols"),
            P("rows", "cols"),
            P("rows", "cols"),
            P("cols"),
            P(None, "rows", "cols"),
            P(None, "cols"),
            P(None, "rows", "cols"),
            P(None, "cols"),
            P("rows", "cols"),
            P("cols"),
            P("rows", "cols"),
            P("cols"),
        ),
        check_vma=False,
    )
```

```python
import jax
import jax.numpy as jnp
from jax import lax
from jax.experimental import pallas as pl
from jax.experimental.pallas import tpu as pltpu
from jax.sharding import PartitionSpec as P

eps = 1e-06
bf16 = jnp.bfloat16
f32 = jnp.float32
MIB = 1 << 20
PLACE = {}


def tie(*arrays):
    return lax.optimization_barrier(arrays)


def gate(arrays, *tokens):
    return list(tie(*arrays, *tokens)[: len(arrays)])


def product(left_side, right_side):
    return jnp.dot(left_side, right_side, preferred_element_type=f32)


def product_t(left_side, right_side):
    return lax.dot_general(
        left_side, right_side, (((0,), (0,)), ((), ())), preferred_element_type=f32
    )


def product_rt(left_side, right_side):
    return lax.dot_general(
        left_side, right_side, (((1,), (1,)), ((), ())), preferred_element_type=f32
    )


def tanh_of(x):
    return jnp.tanh(0.7978845608028654 * (x + 0.044715 * (x * x * x)))


def gelu(x):
    return 0.5 * x * (1.0 + tanh_of(x))


def gelu_grad(x):
    t = tanh_of(x)
    slope = 0.7978845608028654 * (1.0 + 0.134145 * (x * x))
    return 0.5 * (1.0 + t) + 0.5 * x * (1.0 - t * t) * slope


def swap(array, axis, distance):
    size = lax.axis_size(axis)
    return lax.ppermute(array, axis, [(i, i ^ distance) for i in range(size)])


def gather_cols(shard, beside=()):
    size = lax.axis_size("cols")
    far = [swap(shard, "cols", step) for step in range(2, size, 2)]
    if beside:
        tied = tie(*far, *beside)
        far, beside = tied[: len(far)], tied[len(far) :]
    blocks = []
    for block in [shard, *far]:
        blocks += [block, swap(block, "cols", 1)]
    return (blocks, beside) if beside else blocks


def pair_sums(blocks, dot=None):
    evens, odds = blocks[2::2], blocks[3::2]
    came = [swap(odd, "cols", 1) for odd in odds]
    near = [blocks[0], swap(blocks[1], "cols", 1)]
    outs = [(block.shape, bf16) for block in evens]
    if dot is None:
        return near, list(call(pair_kernel, outs, *evens, *came))
    *pairs, dot = call(
        pair_dot_kernel, outs + [(dot.shape, f32)], *evens, *came, dot, swap(dot, "cols", 1)
    )
    return near, pairs, dot


def parts_of(near, pairs, beside=()):
    far = [swap(pair, "cols", 2 * i + 2) for i, pair in enumerate(pairs)]
    parts = tie(*near, *far, *beside)
    count = 2 + len(far)
    return (parts[:count], parts[count:]) if beside else parts


def all_chips(dot):
    return [dot] + [
        swap(dot, "cols", far) for far in range(2, lax.axis_size("cols"), 2)
    ]


def row_exchange(chunks):
    return lax.all_to_all(chunks, "rows", split_axis=0, concat_axis=0, tiled=True)


def row_order():
    return list(reversed(range(lax.axis_size("rows"))))


def exchange(chunks):
    return [
        swap(chunk, "rows", k) if k else chunk for k, chunk in zip(row_order(), chunks)
    ]


class Going:
    def __init__(self, pieces, keep, send, level):
        self.pieces, self.keep, self.level = pieces, keep, level
        self.came = swap(send, "rows", 1 << level)

    def after(self, token):
        self.keep, self.came = gate([self.keep, self.came], token)
        return self


VECTORS = (0, 16)


def halves(pieces):
    return [(n // 2, m) for n, m in pieces]


def rows_of(pieces):
    return sum(n * m if n else m for n, m in pieces)


def fold(*goings):
    pieces = [p for going in goings for p in going.pieces]
    level = goings[0].level + 1
    half = halves(pieces)
    shape = (rows_of(half), goings[0].keep.shape[1])
    arrays = [a for going in goings for a in (going.keep, going.came)]
    kernel = form(fold_kernel, [going.pieces for going in goings], level)
    keep, send = call(kernel, [(shape, bf16)] * 2, *arrays)
    return Going(half, keep, send, level)


def close(going):
    while going.pieces[0][0] > 1:
        going = fold(going)
    total = going.keep.astype(f32) + going.came.astype(f32)
    outs, at = [], 0
    for n, m in going.pieces:
        part = total[at : at + m]
        outs.append(part if n else part[: m // 2] + part[m // 2 :])
        at += m
    return outs


def form(kernel, *options):
    def run(*refs):
        kernel(*options, *refs)

    run.__name__ = kernel.__name__
    return run


def call(kernel, outs, *ins, saved=(), scratch=(), flops=0):
    vmem = pl.BlockSpec(memory_space=pltpu.VMEM)
    shapes = [jax.ShapeDtypeStruct(shape, dtype) for shape, dtype in outs]
    placed = [pltpu.HBM(shape, dtype) for shape, dtype in saved]
    size = sum(a.size * a.dtype.itemsize for a in ins)
    size += sum(jnp.dtype(t).itemsize * n[0] * n[1] for n, t in list(outs) + list(saved))
    extra = sum(jnp.dtype(t).itemsize * n[0] * n[1] for n, t in saved)

    def run(me_ref, *refs):
        if not saved:
            kernel(me_ref, *refs)
            return
        inner = len(ins) + len(outs)
        count = len(saved)
        targets, held = refs[inner : inner + count], refs[inner + count : -1]
        kernel(me_ref, *refs[:inner], *held)
        copies = [
            pltpu.make_async_copy(held[i], targets[i], refs[-1].at[i])
            for i in range(count)
        ]
        for copy in copies:
            copy.start()
        for copy in copies:
            copy.wait()

    return pl.pallas_call(
        run,
        out_shape=shapes + placed,
        in_specs=[pl.BlockSpec(memory_space=pltpu.SMEM)] + [vmem] * len(ins),
        out_specs=[vmem] * len(shapes)
        + [pl.BlockSpec(memory_space=pltpu.HBM)] * len(placed),
        scratch_shapes=[pltpu.VMEM(shape, dtype) for shape, dtype in [*saved, *scratch]]
        + ([pltpu.SemaphoreType.DMA((len(saved),))] if saved else []),
        cost_estimate=pl.CostEstimate(flops=flops, bytes_accessed=size, transcendentals=0),
        compiler_params=pltpu.CompilerParams(
            vmem_limit_bytes=max(12 * MIB, size * 5 // 4 + extra + 6 * MIB)
        ),
        name=kernel.__name__,
    )(PLACE["me"], *ins)


def copy_in(*parts):
    arrays = [part[0] for part in parts]
    count = len(parts)
    shapes = []
    for array, index, rows in parts:
        size = array.shape[-2] if rows is None else rows[1] - rows[0]
        shapes.append(jax.ShapeDtypeStruct((size, array.shape[-1]), array.dtype))

    def run(*refs):
        sems = refs[-1]
        copies = []
        for i, (array, index, rows) in enumerate(parts):
            source = refs[i] if index is None else refs[i].at[index]
            if rows is not None:
                source = source.at[pl.ds(rows[0], rows[1] - rows[0])]
            copies.append(pltpu.make_async_copy(source, refs[count + i], sems.at[i]))
        for copy in copies:
            copy.start()
        for copy in copies:
            copy.wait()

    size = sum(s.size * s.dtype.itemsize for s in shapes)
    return pl.pallas_call(
        run,
        out_shape=shapes,
        in_specs=[pl.BlockSpec(memory_space=pltpu.HBM)] * count,
        out_specs=[pl.BlockSpec(memory_space=pltpu.VMEM)] * count,
        scratch_shapes=[pltpu.SemaphoreType.DMA((count,))],
        cost_estimate=pl.CostEstimate(flops=0, bytes_accessed=size, transcendentals=0),
        compiler_params=pltpu.CompilerParams(vmem_limit_bytes=size * 2 + 4 * MIB),
    )(*[pltpu.with_memory_space_constraint(a, pltpu.HBM) for a in arrays])


def block_rows(me_ref, j, size):
    return pl.ds(pl.multiple_of((me_ref[0] ^ j) * size, size), size)


def sum_refs(refs):
    total = refs[0][...].astype(f32)
    for ref in refs[1:]:
        total = total + ref[...].astype(f32)
    return total


def blocks_product(me_ref, block_refs, weight_ref):
    total = None
    for j, ref in enumerate(block_refs):
        rows = block_rows(me_ref, j, ref.shape[1])
        term = product(ref[...], weight_ref[rows, :])
        total = term if total is None else total + term
    return total


def blocks_scale(block_refs):
    total = None
    for ref in block_refs:
        wide = ref[...].astype(f32)
        term = jnp.sum(wide * wide, axis=1, keepdims=True)
        total = term if total is None else total + term
    return lax.rsqrt(total / (len(block_refs) * block_refs[0].shape[1]) + eps)


def lane_mask():
    return lax.broadcasted_iota(jnp.int32, (128, 128), 0) == lax.broadcasted_iota(
        jnp.int32, (128, 128), 1
    )


def to_lanes(column, out_ref):
    mask = lane_mask()
    for i in range(out_ref.shape[0]):
        part = jnp.where(mask, column[i * 128 : (i + 1) * 128], 0.0)
        out_ref[i : i + 1, :] = jnp.sum(part, axis=0, keepdims=True)


def from_lanes(rows):
    mask = lane_mask()
    return jnp.concatenate(
        [
            jnp.sum(jnp.where(mask, rows[i : i + 1, :], 0.0), axis=1, keepdims=True)
            for i in range(rows.shape[0])
        ],
        axis=0,
    )


def pair_kernel(me_ref, *refs):
    count = len(refs) // 3
    for one, other, out in zip(refs[:count], refs[count : 2 * count], refs[2 * count :]):
        out[...] = (one[...].astype(f32) + other[...].astype(f32)).astype(bf16)


def pair_dot_kernel(me_ref, *refs):
    count = (len(refs) - 3) // 3
    blocks, rest = refs[: 2 * count], refs[2 * count :]
    pair_kernel(me_ref, *blocks, *rest[2 : 2 + count])
    rest[-1][...] = rest[0][...] + rest[1][...]


def flat_kernel(me_ref, dense, out):
    nodes = out.shape[0]
    groups = dense.shape[0] // nodes
    for h in range(groups):
        part = dense[pl.ds(h, nodes, stride=groups), :]
        out[:, h * 128 : (h + 1) * 128] = part.astype(bf16)


def counts_kernel(me_ref, own, other, out, out_t):
    core = me_ref[0] & 1
    size = own.shape[0]
    for ref, place in ((own, core), (other, 1 - core)):
        rows = pl.ds(pl.multiple_of(place * size, size), size)
        value = ref[...]
        out[rows, :] = value
        out_t[:, rows] = value.T


def board_kernel(count, save, me_ref, *refs):
    blocks, refs = refs[:count], refs[count:]
    weight, bias, *refs = refs
    pre = blocks_product(me_ref, blocks, weight) + bias[...]
    if save:
        refs[0][...] = pre
        return
    pin, kinds, hidden_out = refs
    board = from_lanes(kinds) > 0.5
    hidden_out[...] = jnp.where(board, gelu(pre), pin[...].astype(f32)).astype(bf16)


def chunk_span(me_ref, k, size):
    return pl.ds(pl.multiple_of((me_ref[1] ^ k) * size, size), size)


def send_chunks(me_ref, matrix, value, outs, first):
    for i, out in enumerate(outs):
        rows = chunk_span(me_ref, first - i, out.shape[0])
        out[...] = product(matrix[rows, :], value).astype(bf16)


def rest_kernel(me_ref, value, matrix, *outs):
    send_chunks(me_ref, matrix, value[...], outs, len(outs) - 1)


def take_chunks(me_ref, matrix, chunks):
    total = None
    for k, ref in zip(reversed(range(len(chunks))), chunks):
        term = product(matrix[:, chunk_span(me_ref, k, ref.shape[0])], ref[...])
        total = term if total is None else total + term
    return total


def neigh_kernel(count, scaled, me_ref, *refs):
    blocks, refs = refs[:count], refs[count:]
    weight, bias, selector, moved_out, *outs = refs
    pre = blocks_product(me_ref, blocks, weight)
    if scaled:
        pre = blocks_scale(blocks) * pre
    moved = gelu(pre + bias[...]).astype(bf16)
    moved_out[...] = moved
    send_chunks(me_ref, selector, moved, outs, 2 * len(outs) - 1)


def neigh_save_kernel(count, scaled, me_ref, *refs):
    blocks, refs = refs[:count], refs[count:]
    weight, bias, self_w, self_out, pre_out, *refs = refs
    raw = blocks_product(me_ref, blocks, weight)
    if scaled:
        scale_out, raw_out = refs
        scale = blocks_scale(blocks)
        to_lanes(scale, scale_out)
        raw_out[...] = raw
        pre_out[...] = scale * raw + bias[...]
    else:
        pre_out[...] = raw + bias[...]
    self_out[...] = blocks_product(me_ref, blocks, self_w)


def aggregate_kernel(count, me_ref, *refs):
    chunks, (counts, inv_total, out) = refs[:count], refs[count:]
    total = take_chunks(me_ref, counts, chunks)
    out[...] = (total * from_lanes(inv_total)).astype(bf16)


def combine_kernel(count, scaled, save, me_ref, *refs):
    blocks, refs = refs[:count], refs[count:]
    weight, bias, self_raw, *refs = refs
    pre = blocks_product(me_ref, blocks, weight)
    own = self_raw[...]
    if scaled:
        own = from_lanes(refs[0]) * own
    pre = own + pre + bias[...]
    if save:
        refs[-1][...] = pre
    else:
        refs[-1][...] = gelu(pre).astype(bf16)


def blocks_rt(me_ref, pairs, outs):
    for j in reversed(range(len(outs))):
        rows = block_rows(me_ref, j, outs[j].shape[1])
        total = None
        for g, w in pairs:
            term = product_rt(g, w[rows, :])
            total = term if total is None else total + term
        outs[j][...] = total.astype(bf16)


def rt_kernel(me_ref, grad, weight, *outs):
    blocks_rt(me_ref, [(grad[...], weight)], outs)


def head_kernel(count, me_ref, *refs):
    blocks, refs = refs[:count], refs[count:]
    parts, refs = refs[: count // 2 + 1], refs[count // 2 + 1 :]
    weight, bias, *outs = refs
    outs, (dot_out, grad_out, scale_out, inner_out) = outs[:count], outs[count:]
    raw = blocks_product(me_ref, blocks, weight)
    scale = blocks_scale(blocks)
    to_lanes(scale, scale_out)
    pre = scale * raw + bias[...]
    inner_out[...] = gelu(pre).astype(bf16)
    grad = (sum_refs(parts) * gelu_grad(pre)).astype(bf16)
    grad_out[...] = grad
    blocks_rt(me_ref, [(grad, weight)], outs)
    to_lanes(jnp.sum(raw * grad.astype(f32), axis=1, keepdims=True), dot_out)


def combine_back_kernel(count, width, me_ref, *refs):
    parts, refs = refs[: count // 2 + 1], refs[count // 2 + 1 :]
    dots, refs = refs[: count // 2], refs[count // 2 :]
    weight, scale, pre, *outs, grad_out = refs
    dot = sum_refs(dots)
    scale, pre = from_lanes(scale), pre[...]
    factor = scale * scale * scale * from_lanes(dot) / width
    act_grad = scale * sum_refs(parts) - gelu(pre) * factor
    grad = (act_grad * gelu_grad(pre)).astype(bf16)
    grad_out[...] = grad
    blocks_rt(me_ref, [(grad, weight)], outs)


def pool_back_kernel(count, me_ref, *refs):
    parts, refs = refs[: count // 2 + 1], refs[count // 2 + 1 :]
    counts_t, inv_total, grad_out, *outs = refs
    grad = (sum_refs(parts) * from_lanes(inv_total)).astype(bf16)
    grad_out[...] = grad
    send_chunks(me_ref, counts_t, grad, outs, 2 * len(outs) - 1)


def neigh_back_kernel(count, cols, dotted, me_ref, *refs):
    chunks, refs = refs[:count], refs[count:]
    select_t, pre, combine_grad, self_w, weight, *refs = refs
    grad = (take_chunks(me_ref, select_t, chunks) * gelu_grad(pre[...])).astype(bf16)
    own = combine_grad[...]
    if dotted:
        self_raw, raw, *refs = refs
        dot = self_raw[...] * own.astype(f32) + raw[...] * grad.astype(f32)
        to_lanes(jnp.sum(dot, axis=1, keepdims=True), refs[-1])
    refs[cols][...] = grad
    blocks_rt(me_ref, [(own, self_w), (grad, weight)], refs[:cols])


def board_back_kernel(count, row_count, me_ref, *refs):
    parts, refs = refs[: count // 2 + 1], refs[count // 2 + 1 :]
    blocks, refs = refs[:count], refs[count:]
    pre, kinds, *biases = refs
    biases, (keep, send, sums, grad_out) = biases[:6], biases[6:]
    board = from_lanes(kinds) > 0.5
    wide = jnp.where(board, sum_refs(parts), 0.0) * gelu_grad(pre[...])
    grad = wide.astype(bf16)
    grad_out[...] = grad
    rows = keep.shape[0] - 16
    terms_kernel(
        [(count, False)],
        row_count,
        False,
        me_ref,
        *blocks,
        grad,
        keep.at[pl.ds(0, rows)],
        send.at[pl.ds(0, rows)],
        sums,
    )
    last = sums[...]
    stacked = [ref[...] for ref in biases] + [last, jnp.zeros_like(last)]
    stacked = split_vectors(jnp.concatenate(stacked, axis=0))
    keep[rows : rows + 16, :] = stacked
    send[rows : rows + 16, :] = stacked


def board_rest_kernel(count, me_ref, *refs):
    parts, (kinds, grad, weight, *refs) = refs[: count // 2 + 1], refs[count // 2 + 1 :]
    outs, (pin_out,) = refs[:count], refs[count:]
    blocks_rt(me_ref, [(grad[...], weight)], outs)
    pin_out[...] = jnp.where(from_lanes(kinds) > 0.5, 0.0, sum_refs(parts))


def place_piece(stay, keep, send, at, value):
    rows = pl.ds(pl.multiple_of(at, 16), value.shape[0])

    @pl.when(stay)
    def _():
        keep[rows, :] = value

    @pl.when(jnp.logical_not(stay))
    def _():
        send[rows, :] = value


def terms_kernel(sets, row_count, joined, me_ref, *refs):
    *refs, keep, send, sum_out = refs
    count = sum(n for n, _ in sets)
    blocks, refs = refs[:count], refs[count:]
    if joined:
        rows = sum(ref.shape[1] for ref in blocks) // 2
        for other, out in zip(refs[-2:], (keep, send)):
            out[pl.ds(rows, other.shape[0]), :] = other[...]
    grad = refs[0][...]
    wide = grad.astype(f32)
    sum_out[...] = jnp.sum(wide, axis=0, keepdims=True)
    total = sum(ref.shape[1] for ref in blocks)
    chunk = total // row_count
    bit = me_ref[1] & 1
    base = 0
    for n, scaled in sets:
        value = (from_lanes(refs[1]) * wide).astype(bf16) if scaled else grad
        for j in range(n):
            ref = blocks[j]
            size = ref.shape[1]
            part = product_t(ref[...], value).astype(bf16)
            step = min(size, chunk)
            first = base + (me_ref[0] ^ j) * size
            for i in range(size // step):
                start = first + i * step
                q = start // chunk
                at = (q // 2) * chunk + start % chunk
                stay = (q & 1) == bit
                place_piece(stay, keep, send, at, part[i * step : (i + 1) * step])
        base += sum(ref.shape[1] for ref in blocks[:n])
        blocks = blocks[n:]


def turn_kernel(count, me_ref, *refs):
    for blocks, out in zip(
        [refs[i : i + count] for i in range(0, len(refs) - len(refs) // (count + 1), count)],
        refs[-(len(refs) // (count + 1)) :],
    ):
        for j, ref in enumerate(blocks):
            out[block_rows(me_ref, j, ref.shape[1]), :] = ref[...].T


def turned_kernel(scaled, row_count, joined, me_ref, *refs):
    *refs, keep, send, sum_out = refs
    arrays, refs = refs[: len(scaled)], refs[len(scaled) :]
    rows = sum(ref.shape[0] for ref in arrays) // 2
    if joined:
        for other, out in zip(refs[-2:], (keep, send)):
            out[pl.ds(rows, other.shape[0]), :] = other[...]
    grad = refs[0][...]
    wide = grad.astype(f32)
    sum_out[...] = jnp.sum(wide, axis=0, keepdims=True)
    chunk = 2 * rows // row_count
    bit = me_ref[1] & 1
    base = 0
    for ref, by_scale in zip(arrays, scaled):
        value = (from_lanes(refs[1]) * wide).astype(bf16) if by_scale else grad
        step = 2 * chunk
        for p in range(ref.shape[0] // step):
            at = base + p * chunk
            for out, place in ((keep, bit), (send, 1 - bit)):
                span = pl.ds(pl.multiple_of(p * step + place * chunk, 16), chunk)
                out[at : at + chunk, :] = product(ref[span, :], value).astype(bf16)
        base += ref.shape[0] // 2


def tail_kernel(count, row_count, me_ref, *refs):
    blocks, refs = refs[:count], refs[count:]
    weight, bias, cotangent, keep, send, sum_out, out = refs
    out[...] = blocks_product(me_ref, blocks, weight) + bias[...]
    terms_kernel(
        [(count, False)],
        row_count,
        False,
        me_ref,
        *blocks,
        cotangent,
        keep,
        send,
        sum_out,
    )


def split_vectors(values):
    high = values.astype(bf16).astype(f32)
    return jnp.concatenate([high, values - high], axis=0).astype(bf16)


def fold_kernel(groups, level, me_ref, *refs):
    *refs, keep, send = refs
    bit = (me_ref[1] >> level) & 1
    base = 0
    for i, pieces in enumerate(groups):
        one, other = refs[2 * i], refs[2 * i + 1]
        at = 0
        for n, m in pieces:
            if n == 0:
                span = slice(at, at + m)
                total = one[span, :].astype(f32) + other[span, :].astype(f32)
                total = split_vectors(total[: m // 2] + total[m // 2 :])
                keep[base : base + m, :] = total
                send[base : base + m, :] = total
                at += m
                base += m
            for q in range(0, n, 2):
                rows = slice(base + (q // 2) * m, base + (q // 2 + 1) * m)
                for out, place in ((keep, bit), (send, 1 - bit)):
                    span = pl.ds(pl.multiple_of(at + (q + place) * m, 16), m)
                    total = one[span, :].astype(f32) + other[span, :].astype(f32)
                    out[rows, :] = total.astype(bf16)
            at += n * m
            base += (n // 2) * m


def dense_counts(neighbours, visit_counts, pool_size):
    low_width = 128
    high_width = pool_size // low_width
    upper_idx = neighbours // low_width
    lower_idx = neighbours % low_width
    upper_hot = jnp.where(
        upper_idx[:, :, None] == jnp.arange(high_width, dtype=jnp.int32)[None, None, :],
        visit_counts[:, :, None],
        0,
    ).astype(bf16)
    lower_hot = (
        lower_idx[:, :, None] == jnp.arange(low_width, dtype=jnp.int32)[None, None, :]
    ).astype(bf16)
    dense = jnp.einsum("vkh,vkl->vhl", upper_hot, lower_hot, preferred_element_type=f32)
    return dense.reshape(-1, low_width)


def body(
    pin_feats,
    board_feats,
    node_kinds,
    neighbours,
    visit_counts,
    pull_rows,
    proj_weight,
    proj_bias,
    neigh_weight,
    neigh_bias,
    combine_weight,
    combine_bias,
    head_weight,
    head_bias,
    tail_weight,
    tail_bias,
    cotangent,
):
    row_count = lax.axis_size("rows")
    cols = lax.axis_size("cols")
    PLACE["me"] = jnp.stack([lax.axis_index("cols"), lax.axis_index("rows")]).astype(
        jnp.int32
    )
    pool_size = pull_rows.shape[1]
    capacity = pool_size // row_count
    nodes, channels = pin_feats.shape
    width = neigh_weight.shape[1]
    square = 2 * nodes * width * channels
    spread_flops = 2 * nodes * pool_size * channels
    block = (nodes, channels)
    lanes = (nodes // 128, 128)
    middle = row_count // 2
    half_outs = [((capacity, channels), bf16)] * (row_count // 2)
    block_outs = [(block, bf16)] * cols
    row_vector = ((1, channels), f32)

    def term_halves(sets, blocks, grad, scale=None, joined=None):
        rows = sum(b.shape[1] for b in blocks)
        pieces, others = ([], ()) if joined is None else joined
        pieces = [(row_count // 2, rows // row_count), *pieces]
        keep, send, sums = call(
            form(terms_kernel, sets, row_count, joined is not None),
            [((rows_of(pieces), channels), bf16)] * 2 + [row_vector],
            *blocks,
            grad,
            *(() if scale is None else (scale,)),
            *others,
            flops=2 * nodes * rows * channels,
        )
        return pieces, [keep, send], sums

    def terms(*args, joined=None):
        pieces, halves_of, sums = term_halves(*args, joined=joined)
        return Going(pieces, *halves_of, 0), sums

    def turn(*runs):
        return call(
            form(turn_kernel, cols),
            [((sum(b.shape[1] for b in run), nodes), bf16) for run in runs],
            *[b for run in runs for b in run],
        )

    def turned_halves(scaled, arrays, grad, scale=None, joined=None):
        rows = sum(a.shape[0] for a in arrays)
        pieces, others = ([], ()) if joined is None else joined
        pieces = [(row_count // 2, rows // row_count), *pieces]
        keep, send, sums = call(
            form(turned_kernel, scaled, row_count, joined is not None),
            [((rows_of(pieces), channels), bf16)] * 2 + [row_vector],
            *arrays,
            grad,
            *(() if scale is None else (scale,)),
            *others,
            flops=2 * nodes * rows * channels,
        )
        return pieces, [keep, send], sums

    def turned_terms(*args, joined=None):
        pieces, halves_of, sums = turned_halves(*args, joined=joined)
        return Going(pieces, *halves_of, 0), sums

    def both_halves(matrix, first):
        value, *sent = first
        rest = call(rest_kernel, half_outs, value, matrix, flops=spread_flops // 2)
        return sent + list(rest)

    requested = row_exchange(pull_rows.reshape(row_count, capacity)).reshape(-1)
    board_blocks = gather_cols(board_feats)
    kinds = (node_kinds == 1).astype(f32).reshape(lanes)
    proj_in, proj_bias_in, pins = copy_in(
        (proj_weight, None, None), (proj_bias[None], None, None), (pin_feats, None, None)
    )
    (hidden,) = call(
        form(board_kernel, cols, False),
        [(block, bf16)],
        *board_blocks,
        proj_in,
        proj_bias_in,
        pins,
        kinds,
        flops=square // 2,
    )
    hidden, requested = tie(hidden, requested)
    share = nodes // 2
    counted, visits = (
        lax.dynamic_slice_in_dim(a, lax.axis_index("cols") % 2 * share, share)
        for a in gate([neighbours, visit_counts], hidden)
    )
    dense = dense_counts(counted, visits, pool_size)
    local = jnp.arange(nodes, dtype=jnp.int32)
    selector = (requested[:, None] == local[None, :]).astype(bf16)
    (neigh_w0,) = copy_in((gate([neigh_weight], hidden)[0], 0, None))
    inv_total = (1.0 / jnp.sum(visit_counts.astype(f32), axis=1)).reshape(lanes)

    blocks_0, (neigh_w0, selector, dense) = gather_cols(
        hidden, (neigh_w0, selector, dense)
    )
    (own_counts,) = call(
        flat_kernel, [((share, pool_size), bf16)], *gate([dense], blocks_0[2])
    )
    *blocks_0, own_counts = tie(*blocks_0, own_counts)
    other_counts = swap(own_counts, "cols", 1)
    sent = both_halves(
        selector,
        call(
            form(neigh_kernel, cols, False),
            [(block, bf16)] + half_outs,
            *blocks_0,
            neigh_w0,
            neigh_bias[0:1],
            selector,
            flops=square + spread_flops // 2,
        ),
    )
    counts, counts_t = call(
        counts_kernel,
        [((nodes, pool_size), bf16), ((pool_size, nodes), bf16)],
        own_counts,
        other_counts,
    )
    (turned_0,) = turn(gate(blocks_0, sent[-1]))
    sent[-2], counts, counts_t, turned_0 = tie(sent[-2], counts, counts_t, turned_0)
    chunks = exchange(sent)
    (gathered,) = call(
        form(aggregate_kernel, row_count),
        [(block, bf16)],
        *chunks,
        counts,
        inv_total,
        flops=spread_flops,
    )
    self_w0, gather_w0, neigh_b, combine_b = copy_in(
        (gate([combine_weight], gathered)[0], 0, (0, width)),
        (combine_weight, 0, (width, 2 * width)),
        (neigh_bias, None, None),
        (combine_bias, None, None),
    )
    self_raw_0, neigh_pre_0 = call(
        form(neigh_save_kernel, cols, False),
        [(block, f32), (block, f32)],
        *gate(blocks_0, gathered),
        neigh_w0,
        neigh_b[0:1],
        self_w0,
        flops=2 * square,
    )
    gathered_0, (self_raw_0, neigh_pre_0, gather_w0) = gather_cols(
        gathered, (self_raw_0, neigh_pre_0, gather_w0)
    )
    fixed = (gather_w0, combine_b[0:1], self_raw_0)
    (act,) = call(
        form(combine_kernel, cols, False, False),
        [(block, bf16)],
        *gathered_0,
        *fixed,
        flops=square,
    )
    (combine_pre_0,) = call(
        form(combine_kernel, cols, False, True),
        [(block, f32)],
        *gate([*gathered_0, *fixed], act),
        flops=square,
    )
    (neigh_w1, *weights) = copy_in(
        (gate([neigh_weight], act)[0], 1, None),
        (combine_weight, 1, (0, width)),
        (combine_weight, 1, (width, 2 * width)),
        (head_weight, None, None),
        (tail_weight, None, None),
        (head_bias[None], None, None),
        (tail_bias[None], None, None),
        (cotangent, None, None),
    )

    blocks_1, (combine_pre_0, neigh_w1, *weights) = gather_cols(
        act, (combine_pre_0, neigh_w1, *weights)
    )
    self_w1, gather_w1, head_w, tail_w, head_b, tail_b, cotangent = weights
    sent = both_halves(
        selector,
        call(
            form(neigh_kernel, cols, True),
            [(block, bf16)] + half_outs,
            *blocks_1,
            neigh_w1,
            neigh_b[1:2],
            selector,
            flops=square + spread_flops // 2,
        ),
    )
    inner_near, pairs = pair_sums(
        call(rt_kernel, block_outs, *gate([cotangent], sent[-1]), tail_w, flops=square)
    )
    inner_parts = parts_of(inner_near, pairs)
    turned_1, turned_gathered_0 = turn(
        gate(blocks_1, sent[-1]), gate(gathered_0, sent[-1])
    )
    sent[-2], turned_1, turned_gathered_0 = tie(sent[-2], turned_1, turned_gathered_0)
    chunks = exchange(sent)
    (gathered,) = call(
        form(aggregate_kernel, row_count),
        [(block, bf16)],
        *chunks,
        counts,
        inv_total,
        flops=spread_flops,
    )
    *late, requested_late = gate([*blocks_1, requested], gathered)
    self_raw_1, neigh_pre_1, scale_1, neigh_raw_1 = call(
        form(neigh_save_kernel, cols, True),
        [(block, f32), (block, f32), (lanes, f32), (block, f32)],
        *late,
        neigh_w1,
        neigh_b[1:2],
        self_w1,
        flops=2 * square,
    )
    select_t = (local[:, None] == requested_late[None, :]).astype(bf16)
    (board_pre,) = call(
        form(board_kernel, cols, True),
        [(block, f32)],
        *gate(board_blocks, gathered),
        proj_in,
        proj_bias_in,
        flops=square // 2,
    )
    gathered_1, (self_raw_1, neigh_pre_1, scale_1, neigh_raw_1, select_t, board_pre) = (
        gather_cols(
            gathered,
            (self_raw_1, neigh_pre_1, scale_1, neigh_raw_1, select_t, board_pre),
        )
    )
    fixed = (gather_w1, combine_b[1:2], self_raw_1, scale_1)
    (act,) = call(
        form(combine_kernel, cols, True, False),
        [(block, bf16)],
        *gathered_1,
        *fixed,
        flops=square,
    )
    (combine_pre_1,) = call(
        form(combine_kernel, cols, True, True),
        [(block, f32)],
        *gate([*gathered_1, *fixed], act),
        flops=square,
    )

    (turned_gathered_1,) = turn(gate(gathered_1, act))
    blocks_2, (combine_pre_1, turned_gathered_1, *inner_parts) = gather_cols(
        act, (combine_pre_1, turned_gathered_1, *inner_parts)
    )
    *blocks, dot, head_grad, scale_2, inner_act = call(
        form(head_kernel, cols),
        block_outs + [(lanes, f32), (block, bf16), (lanes, f32), (block, bf16)],
        *blocks_2,
        *inner_parts,
        head_w,
        head_b,
        flops=3 * square,
    )
    near, pairs, dot = pair_sums(blocks, dot)
    head_going, head_bias_grad = terms(
        [(cols, True)], blocks_2, *gate([head_grad], pairs[0]), scale_2
    )
    parts, (head_going.keep,) = parts_of(near, pairs, (head_going.keep,))
    dots = all_chips(dot)

    def combine_back(parts, dots, weight, scale, pre):
        *blocks, grad = call(
            form(combine_back_kernel, cols, width),
            block_outs + [(block, bf16)],
            *parts,
            *dots,
            weight,
            scale,
            pre,
            flops=square,
        )
        return grad, *pair_sums(blocks)

    def pool_back(parts):
        return both_halves(
            counts_t,
            call(
                form(pool_back_kernel, cols),
                [(block, bf16)] + half_outs,
                *parts,
                counts_t,
                inv_total,
                flops=spread_flops // 2,
            ),
        )

    combine_grad, near, pairs = combine_back(
        parts, dots, gather_w1, scale_2, combine_pre_1
    )
    combine_going, combine_bias_1 = turned_terms(
        (True, False),
        [turned_1, turned_gathered_1],
        *gate([combine_grad], pairs[0]),
        scale_1,
    )
    parts, (combine_going.keep, head_going.came) = parts_of(
        near, pairs, (combine_going.keep, head_going.came)
    )
    sent = pool_back(parts)
    chunks = exchange(sent)
    inner_blocks = gather_cols(*gate([inner_act], sent[-1]))
    *chunks, inner_blocks[-2], combine_going.came = tie(
        *chunks, inner_blocks[-2], combine_going.came
    )

    neigh_in = (select_t, neigh_pre_1, combine_grad, self_w1, neigh_w1)
    *blocks, neigh_grad_1, dot = call(
        form(neigh_back_kernel, row_count, cols, True),
        block_outs + [(block, bf16), (lanes, f32)],
        *chunks,
        *neigh_in,
        self_raw_1,
        neigh_raw_1,
        flops=spread_flops + 2 * square,
    )
    near, pairs, dot = pair_sums(blocks, dot)
    first_going = fold(head_going.after(pairs[0]), combine_going.after(pairs[0]))
    tail_rows = (width // 2, channels)
    tail_keep, tail_send, tail_bias_grad, embeddings = call(
        form(tail_kernel, cols, row_count),
        [(tail_rows, bf16), (tail_rows, bf16), row_vector],
        *gate(inner_blocks, pairs[0]),
        tail_w,
        tail_b,
        cotangent,
        saved=[(block, f32)],
        flops=2 * square,
    )
    pieces_1, halves_1, neigh_bias_1 = turned_halves(
        (True,),
        [turned_1],
        *gate([neigh_grad_1], pairs[0]),
        scale_1,
        joined=([(row_count // 2, width // row_count)], (tail_keep, tail_send)),
    )
    parts, (first_going.keep, halves_1[0]) = parts_of(
        near, pairs, (first_going.keep, halves_1[0])
    )
    dots = all_chips(dot)

    combine_grad, near, pairs = combine_back(
        parts, dots, gather_w0, scale_1, combine_pre_0
    )
    combine_going, combine_bias_0 = turned_terms(
        (False, False),
        [turned_0, turned_gathered_0],
        combine_grad,
        joined=(pieces_1, halves_1),
    )
    parts, (combine_going.keep, first_going.came) = parts_of(
        near, pairs, (combine_going.keep, first_going.came)
    )
    sent = pool_back(parts)
    chunks = exchange(sent)

    neigh_in = (select_t, neigh_pre_0, combine_grad, self_w0, neigh_w0)
    *blocks, neigh_grad = call(
        form(neigh_back_kernel, row_count, cols, False),
        block_outs + [(block, bf16)],
        *chunks,
        *neigh_in,
        flops=spread_flops + 2 * square,
    )
    near, pairs = pair_sums(blocks)
    first_going = fold(first_going.after(pairs[0]))
    second_going = fold(combine_going.after(pairs[0]))
    neigh_going_0, neigh_bias_0 = turned_terms(
        (False,), [turned_0], *gate([neigh_grad], pairs[0])
    )
    parts, (second_going.keep, neigh_going_0.keep, first_going.keep) = parts_of(
        near, pairs, (second_going.keep, neigh_going_0.keep, first_going.keep)
    )

    board_block = ((nodes, board_feats.shape[1]), bf16)
    proj_rows = proj_weight.shape[0]
    pieces = [(row_count // 2, proj_rows // row_count), VECTORS]
    keep, send, _, board_grad = call(
        form(board_back_kernel, cols, row_count),
        [((rows_of(pieces), channels), bf16)] * 2 + [row_vector, (block, bf16)],
        *parts,
        *board_blocks,
        board_pre,
        kinds,
        neigh_bias_0,
        neigh_bias_1,
        combine_bias_0,
        combine_bias_1,
        head_bias_grad,
        tail_bias_grad,
        flops=square // 2,
    )
    proj_going = Going(pieces, keep, send, 0)
    last_going = fold(neigh_going_0.after(keep), proj_going)
    last_going.came, second_going.came = tie(last_going.came, second_going.came)
    third_going = fold(second_going)
    *blocks, grad_pin = call(
        form(board_rest_kernel, cols),
        [board_block] * cols,
        *gate(parts, last_going.came, third_going.keep),
        kinds,
        board_grad,
        proj_in,
        saved=[(block, f32)],
        flops=square // 2,
    )
    near, pairs = pair_sums(blocks)
    grad_board = sum(p.astype(f32) for p in parts_of(near, pairs))
    third_going.came, grad_board = tie(third_going.came, grad_board)
    head_out, combine_out_1 = close(first_going)
    combine_out_0, neigh_out_1, tail_out = close(third_going)
    neigh_out_0, proj_out, biases = close(last_going)
    return (
        embeddings,
        grad_pin,
        grad_board,
        proj_out,
        biases[6],
        jnp.stack([neigh_out_0, neigh_out_1]),
        biases[0:2],
        jnp.stack([combine_out_0, combine_out_1]),
        biases[2:4],
        head_out,
        biases[4],
        tail_out,
        biases[5],
    )


def solution(mesh):
    placed = (
        P("rows", "cols"),
        P("rows", "cols"),
        P("rows"),
        P("rows", None),
        P("rows", None),
        P("rows", None),
        P(None, "cols"),
        P("cols"),
        P(None, None, "cols"),
        P(None, "cols"),
        P(None, None, "cols"),
        P(None, "cols"),
        P(None, "cols"),
        P("cols"),
        P(None, "cols"),
        P("cols"),
        P("rows", "cols"),
    )
    return jax.shard_map(
        body,
        mesh=mesh,
        in_specs=placed,
        out_specs=(
            P("rows", "cols"),
            P("rows", "cols"),
            P("rows", "cols"),
            P("rows", "cols"),
            P("cols"),
            P(None, "rows", "cols"),
            P(None, "cols"),
            P(None, "rows", "cols"),
            P(None, "cols"),
            P("rows", "cols"),
            P("cols"),
            P("rows", "cols"),
            P("cols"),
        ),
        check_vma=False,
    )
```
